256 devices in a mesh: blk: 16 (over y, x_hi, core), head: 8 (over z), rep: 2 (over x_lo).
Axes of the slice: x: 4 (x_hi: 2, x_lo: 2; x = x_hi * 2 + x_lo), y: 4, z: 8, core: 2. Of those that a mesh axis runs over, the one named last changes fastest.
Arguments:
- video_q: bfloat16 [32768, 3072], P(('blk', 'head', 'rep')), may hold values from -6 to 6
- video_k: bfloat16 [32768, 3072], P(('blk', 'head', 'rep')), may hold values from -6 to 6
- video_v: bfloat16 [32768, 3072], P(('blk', 'head', 'rep')), may hold values from -15 to 15
- text_q: bfloat16 [512, 3072], P(('blk', 'rep'), 'head'), may hold values from -6 to 6
- text_k: bfloat16 [512, 3072], P(('blk', 'rep'), 'head'), may hold values from -6 to 6
- text_v: bfloat16 [512, 3072], P(('blk', 'rep'), 'head'), may hold values from -15 to 15
- gain_video_q: float32 [128], replicated, may hold values from 1.5 to 2.4
- gain_video_k: float32 [128], replicated, may hold values from 1.5 to 2.4
- gain_text_q: float32 [128], replicated, may hold values from 1.5 to 2.4
- gain_text_k: float32 [128], replicated, may hold values from 1.5 to 2.4
- window: int32 [4], replicated, may hold values from 0 to 255
- grad_out_video: bfloat16 [512, 3072], P(('blk', 'rep'), 'head'), may hold values from -6 to 6
- grad_out_text: bfloat16 [512, 3072], P(('blk', 'rep'), 'head'), may hold values from -6 to 6
Outputs:
- out_video: bfloat16 [512, 3072], P(('blk', 'rep'), 'head')
- out_text: bfloat16 [512, 3072], P(('blk', 'rep'), 'head')
- grad_window_q: bfloat16 [512, 3072], P(('blk', 'rep'), 'head')
- grad_text_q: bfloat16 [512, 3072], P(('blk', 'rep'), 'head')
- grad_video_k: bfloat16 [32768, 3072], P(('blk', 'head', 'rep'))
- grad_video_v: bfloat16 [32768, 3072], P(('blk', 'head', 'rep'))
- grad_text_k: bfloat16 [512, 3072], P(('blk', 'rep'), 'head')
- grad_text_v: bfloat16 [512, 3072], P(('blk', 'rep'), 'head')
The draws below stay inside these ranges and needn't reach their ends.
Inputs may be any that keep to these rules, and one draw needn't show every extreme that they name: `window`: each entry names a block of 128 video rows; entries may repeat.
All inputs are finite; a program needn't handle non-finite values.
Results may differ from the reference program's by a relative error of at most 0.018.
Values may be sent and summed in bfloat16 or wider, within the bound.
No kernel may reach another device: no remote copies, remote signals or barrier semaphores. Data moves between devices by JAX's collectives and lax.ppermute only.
A program may use at most 64 MiB of HBM per device.

```python
import math
import jax
import jax.numpy as jnp
from jax import lax

HEADS = 24
HD = 128
D = 3072
QBLK = 128
NWIN = 4
TEXT = 512
VIDEO = 32768


def set_ends(drawn, key, least, largest):
    spot = [jax.random.randint(jax.random.fold_in(key, axis), (), 0, length) for axis, length in enumerate(drawn.shape)]
    widest = drawn.shape.index(max(drawn.shape))
    next_to = spot[:widest] + [(spot[widest] + 1) % drawn.shape[widest]] + spot[widest + 1:]
    return drawn.at[tuple(spot)].set(least).at[tuple(next_to)].set(largest)


def shard_levels(stream_key, extent, split, smallest, top_value):
    factor_of = 1.0
    for axis_at, parts in split:
        steps = jax.random.uniform(jax.random.fold_in(jax.random.fold_in(stream_key, 6), axis_at), (parts,), jnp.float32, smallest / len(split), top_value / len(split))
        factor_of = factor_of * jnp.repeat(jnp.exp(steps), extent[axis_at] // parts).reshape((-1,) + (1,) * (len(extent) - 1 - axis_at))
    return factor_of


def centred(stream_key, dims, deviation, bound, shards=(), held_as=jnp.bfloat16):
    array = jax.random.normal(stream_key, dims, jnp.float32) * deviation
    if len(shards) > 0:
        array = shard_levels(stream_key, dims, shards, -0.22, 0.18) * array
    return jnp.clip(array, min=-bound, max=bound).astype(held_as)


def setup_inputs(seed: int = 0) -> dict:
    splits = jax.random.split(jax.random.key(seed), 14)
    return {
        "video_q": centred(splits[0], (VIDEO, D), 1.0, 6.0, ((0, 256),)),
        "video_k": centred(splits[1], (VIDEO, D), 1.0, 6.0, ((0, 256),)),
        "video_v": centred(splits[2], (VIDEO, D), 2.5, 15.0, ((0, 256),)),
        "text_q": centred(splits[3], (TEXT, D), 1.0, 6.0, ((0, 32), (1, 8))),
        "text_k": centred(splits[4], (TEXT, D), 1.0, 6.0, ((0, 32), (1, 8))),
        "text_v": centred(splits[5], (TEXT, D), 2.5, 15.0, ((0, 32), (1, 8))),
        "gain_video_q": jnp.clip(jnp.exp(jax.random.uniform(splits[6], (HD,), jnp.float32, math.log(1.5), math.log(2.4))), 1.5, 2.4),
        "gain_video_k": jnp.clip(jnp.exp(jax.random.uniform(splits[7], (HD,), jnp.float32, math.log(1.5), math.log(2.4))), 1.5, 2.4),
        "gain_text_q": jnp.clip(jnp.exp(jax.random.uniform(splits[8], (HD,), jnp.float32, math.log(1.5), math.log(2.4))), 1.5, 2.4),
        "gain_text_k": jnp.clip(jnp.exp(jax.random.uniform(splits[9], (HD,), jnp.float32, math.log(1.5), math.log(2.4))), 1.5, 2.4),
        "window": set_ends(jax.random.randint(splits[10], (NWIN,), 0, VIDEO // QBLK), jax.random.fold_in(splits[10], 1), 0, (VIDEO // QBLK) - 1).astype(jnp.int32),
        "grad_out_video": centred(splits[11], (NWIN * QBLK, D), 1.0, 6.0, ((0, 32), (1, 8))),
        "grad_out_text": centred(splits[12], (TEXT, D), 1.0, 6.0, ((0, 32), (1, 8))),
    }


NORM_EPSILON = 1e-06

def head_norm(flat_rows, gain_vec):
    row_count = flat_rows.shape[0]
    per_head = flat_rows.reshape(row_count, -1, gain_vec.shape[0])
    inverse = lax.rsqrt(lax.optimization_barrier(jnp.mean(per_head * per_head, axis=-1, keepdims=True)) + NORM_EPSILON)
    return (per_head * inverse * gain_vec).reshape(row_count, -1)

def norm_pullback(raw_rows, gain_vec, cotangent):
    _, pullback = jax.vjp(lambda inner_rows: head_norm(inner_rows, gain_vec), raw_rows.astype(jnp.float32))
    return pullback(cotangent)[0]

def reference(video_q, video_k, video_v, text_q, text_k, text_v, gain_video_q, gain_video_k, gain_text_q, gain_text_k, window, grad_out_video, grad_out_text):
    blocks = video_q.reshape(VIDEO // QBLK, QBLK, D)
    window_rows = jnp.take(blocks, window.astype(jnp.int32), axis=0).reshape(NWIN * QBLK, D)
    inv_root = 1.0 / math.sqrt(HD)
    window_count = NWIN * QBLK

    def one_head(head_index):

        def columns(matrix):
            return lax.dynamic_slice_in_dim(matrix, head_index * HD, HD, 1)
        raw_window = columns(window_rows)
        raw_text_q = columns(text_q)
        raw_video_k = columns(video_k)
        raw_text_k = columns(text_k)
        queries = jnp.concatenate((head_norm(raw_window.astype(jnp.float32), gain_video_q), head_norm(raw_text_q.astype(jnp.float32), gain_text_q)), axis=0).astype(jnp.bfloat16)
        normed_keys = jnp.concatenate((head_norm(raw_video_k.astype(jnp.float32), gain_video_k), head_norm(raw_text_k.astype(jnp.float32), gain_text_k)), axis=0).astype(jnp.bfloat16)
        values = jnp.concatenate((columns(video_v), columns(text_v)), axis=0)
        cotangent = jnp.concatenate((columns(grad_out_video), columns(grad_out_text)), axis=0)
        weights = jnp.exp(jnp.dot(queries, normed_keys.T, preferred_element_type=jnp.float32) * inv_root)
        denominator = lax.optimization_barrier(jnp.sum(weights, axis=1, keepdims=True))
        numerator = jnp.dot(weights.astype(jnp.bfloat16), values, preferred_element_type=jnp.float32)
        outputs = (numerator / denominator).astype(jnp.bfloat16)
        probabilities = weights / denominator
        grad_values = jnp.dot(probabilities.astype(jnp.bfloat16).T, cotangent, preferred_element_type=jnp.float32)
        dprobs = jnp.dot(cotangent, values.T, preferred_element_type=jnp.float32)
        delta = lax.optimization_barrier(jnp.sum(cotangent.astype(jnp.float32) * outputs.astype(jnp.float32), axis=1, keepdims=True))
        dscores = (probabilities * (dprobs - delta)).astype(jnp.bfloat16)
        dqueries = jnp.dot(dscores, normed_keys, preferred_element_type=jnp.float32) * inv_root
        dkeys = jnp.dot(dscores.T, queries, preferred_element_type=jnp.float32) * inv_root
        grad_query = jnp.concatenate((norm_pullback(raw_window, gain_video_q, dqueries[:window_count]), norm_pullback(raw_text_q, gain_text_q, dqueries[window_count:])), axis=0)
        grad_key = jnp.concatenate((norm_pullback(raw_video_k, gain_video_k, dkeys[:VIDEO]), norm_pullback(raw_text_k, gain_text_k, dkeys[VIDEO:])), axis=0)
        return (outputs, grad_query.astype(jnp.bfloat16), grad_key.astype(jnp.bfloat16), grad_values.astype(jnp.bfloat16))
    outputs, grad_query, grad_key, grad_value = lax.map(one_head, jnp.arange(HEADS, dtype=jnp.int32))

    def merge_heads(stacked):
        return jnp.transpose(stacked, (1, 0, 2)).reshape(stacked.shape[1], HEADS * HD)
    outputs = merge_heads(outputs)
    grad_query = merge_heads(grad_query)
    grad_key = merge_heads(grad_key)
    grad_value = merge_heads(grad_value)
    return (outputs[:window_count], outputs[window_count:], grad_query[:window_count], grad_query[window_count:], grad_key[:VIDEO], grad_value[:VIDEO], grad_key[VIDEO:], grad_value[VIDEO:])
```

```python
import math

import jax
import jax.numpy as jnp
from jax import lax
from jax.experimental import pallas as pl
from jax.experimental.pallas import tpu as pltpu
from jax.sharding import Mesh, PartitionSpec as P

NWIN = 4
HD = 128
EPS = 1e-06
INV_ROOT = 1.0 / math.sqrt(HD)
LOG2E = math.log2(math.e)
PLANE = ("y", "xh", "c", "xl")
CHIPS = ("y", "xh", "xl")
KEY_BLOCK = 256
NT = (((1,), (1,)), ((), ()))
NN = (((1,), (0,)), ((), ()))
TN = (((0,), (0,)), ((), ()))
F32 = jnp.float32
BF16 = jnp.bfloat16


def mm(a, b, dims):
    return lax.dot_general(a, b, dims, preferred_element_type=F32)


def inverse_rms(rows):
    return lax.rsqrt(jnp.mean(rows * rows, axis=-1, keepdims=True) + EPS)


def normed(raw, gain):
    rows = raw.astype(F32)
    return (rows * inverse_rms(rows) * gain).astype(BF16)


def pullback(raw, gain, cot):
    rows = raw.astype(F32)
    inverse = inverse_rms(rows)
    scaled = cot * gain
    along = jnp.mean(rows * scaled, axis=-1, keepdims=True)
    return inverse * (scaled - rows * (inverse * inverse * along))


def normed_queries(win_ref, text_ref, gains_ref):
    return jnp.concatenate(
        (normed(win_ref[...], gains_ref[0:1]), normed(text_ref[...], gains_ref[2:3])), axis=0
    )


def key_parts(k_ref, v_ref, tk_ref, tv_ref, gains_ref):
    parts = []
    for start in range(0, k_ref.shape[0], KEY_BLOCK):
        rows = slice(start, start + KEY_BLOCK)
        parts.append((k_ref[rows], v_ref[rows], gains_ref[1:2], rows))
    parts.append((tk_ref[...], tv_ref[...], gains_ref[3:4], None))
    return parts


def stats_kernel(win_ref, tq_ref, cot_ref, k_ref, v_ref, tk_ref, tv_ref, gains_ref, out_ref):
    queries = normed_queries(win_ref, tq_ref, gains_ref)
    cot = cot_ref[...]
    den = jnp.zeros((1, queries.shape[0]), F32)
    mixed = jnp.zeros((1, queries.shape[0]), F32)
    for raw_key, value, gain, _ in key_parts(k_ref, v_ref, tk_ref, tv_ref, gains_ref):
        key = normed(raw_key, gain)
        weights = jnp.exp2(mm(key, queries, NT) * (INV_ROOT * LOG2E))
        dprobs = mm(value, cot, NT)
        den += jnp.sum(weights, axis=0, keepdims=True)
        mixed += jnp.sum(weights * dprobs, axis=0, keepdims=True)
    out_ref[0, 0:1] = den
    out_ref[0, 1:2] = mixed


def grads_kernel(
    win_ref, tq_ref, cot_ref, k_ref, v_ref, tk_ref, tv_ref, gains_ref, stats_ref,
    rows_ref, dk_ref, dv_ref, dtk_ref, dtv_ref,
):
    queries = normed_queries(win_ref, tq_ref, gains_ref)
    cot = cot_ref[...]
    count = queries.shape[0]
    inv_den = 1.0 / stats_ref[0, 0:1]
    delta = stats_ref[0, 1:2] * inv_den
    out_t = jnp.zeros((HD, count), F32)
    dq_t = jnp.zeros((HD, count), F32)
    for raw_key, value, gain, rows in key_parts(k_ref, v_ref, tk_ref, tv_ref, gains_ref):
        key = normed(raw_key, gain)
        probs = jnp.exp2(mm(key, queries, NT) * (INV_ROOT * LOG2E)) * inv_den
        probs_16 = probs.astype(BF16)
        dvalue = mm(probs_16, cot, NN).astype(BF16)
        out_t += mm(value, probs_16, TN)
        dscores = (probs * (mm(value, cot, NT) - delta)).astype(BF16)
        dkey = pullback(raw_key, gain, mm(dscores, queries, NN) * INV_ROOT).astype(BF16)
        dq_t += mm(key, dscores, TN)
        if rows is None:
            dtk_ref[...] = dkey
            dtv_ref[...] = dvalue
        else:
            dk_ref[rows] = dkey
            dv_ref[rows] = dvalue
    half = count // 2
    outs = out_t.T.astype(BF16)
    dqs = (dq_t * INV_ROOT).T.astype(BF16)
    groups, part = rows_ref.shape[0], rows_ref.shape[1] // 4
    for place, block in enumerate((outs[:half], outs[half:], dqs[:half], dqs[half:])):
        rows_ref[:, place * part : (place + 1) * part] = block.reshape(groups, part, HD)


def column_spec(array):
    return pl.BlockSpec((array.shape[0], HD), lambda head: (0, head))


def whole_spec(array):
    return pl.BlockSpec(array.shape, lambda head: (0,) * array.ndim)


PARAMS = pltpu.CompilerParams(vmem_limit_bytes=48 * 1024 * 1024)


def attention_stats(operands, gains, heads):
    count = operands[2].shape[0]
    keys = operands[3].shape[0]
    return pl.pallas_call(
        stats_kernel,
        grid=(heads,),
        in_specs=[column_spec(a) for a in operands] + [whole_spec(gains)],
        out_specs=pl.BlockSpec((1, 2, count), lambda head: (head, 0, 0)),
        out_shape=jax.ShapeDtypeStruct((heads, 2, count), F32),
        compiler_params=PARAMS,
        cost_estimate=pl.CostEstimate(
            flops=4 * count * keys * heads * HD, bytes_accessed=6000000,
            transcendentals=count * keys * heads,
        ),
    )(*operands, gains)


def attention_grads(operands, gains, stats, heads, groups):
    count = operands[2].shape[0]
    keys = operands[3].shape[0]
    text = operands[5].shape[0]
    part = count // groups * 2
    width = heads * HD
    shapes = [
        jax.ShapeDtypeStruct((groups, part, width), BF16),
        jax.ShapeDtypeStruct((keys, width), BF16),
        jax.ShapeDtypeStruct((keys, width), BF16),
        jax.ShapeDtypeStruct((text, width), BF16),
        jax.ShapeDtypeStruct((text, width), BF16),
    ]
    return pl.pallas_call(
        grads_kernel,
        grid=(heads,),
        in_specs=[column_spec(a) for a in operands]
        + [whole_spec(gains), pl.BlockSpec((1, 2, count), lambda head: (head, 0, 0))],
        out_specs=[pl.BlockSpec((groups, part, HD), lambda head: (0, 0, head))]
        + [column_spec(s) for s in shapes[1:]],
        out_shape=shapes,
        compiler_params=PARAMS,
        cost_estimate=pl.CostEstimate(
            flops=12 * count * keys * heads * HD, bytes_accessed=9000000,
            transcendentals=count * keys * heads,
        ),
    )(*operands, gains, stats)


def swap(array, axes):
    return lax.all_to_all(array, axes, split_axis=0, concat_axis=0, tiled=True)


def split_heads(rows, groups):
    count = rows.shape[0]
    return rows.reshape(count, groups, -1).transpose(1, 0, 2)


def pick(array, index):
    return lax.dynamic_index_in_dim(array, index, 0, keepdims=False)


def local(
    video_q, video_k, video_v, text_q, text_k, text_v,
    gain_video_q, gain_video_k, gain_text_q, gain_text_k,
    window, grad_out_video, grad_out_text,
):
    z_size = lax.axis_size("z")
    rep_size = lax.axis_size("xl")
    groups = lax.axis_size(PLANE)
    own_rows, model = video_q.shape
    columns = model // z_size
    heads = columns // HD
    share = grad_out_video.shape[0]
    gains = jnp.stack((gain_video_q, gain_video_k, gain_text_q, gain_text_k))

    piece = own_rows // groups
    scattered = swap(video_q.reshape(groups, piece, model), PLANE)
    z_of = [window[s] // rep_size % z_size for s in range(NWIN)]
    plane_of = [
        window[s] // (z_size * rep_size) * rep_size + window[s] % rep_size for s in range(NWIN)
    ]
    picked = jnp.concatenate([pick(scattered, plane_of[s]) for s in range(NWIN)], axis=0)

    sent = jnp.concatenate(
        (
            split_heads(video_k, z_size),
            split_heads(video_v, z_size),
            split_heads(picked, z_size),
        ),
        axis=1,
    )
    moved = swap(sent, "z")
    moved_k = moved[:, :own_rows].reshape(-1, columns)
    moved_v = moved[:, own_rows : 2 * own_rows].reshape(-1, columns)
    moved_q = moved[:, 2 * own_rows :].reshape(z_size, NWIN, piece, columns)
    own_window = jnp.concatenate([pick(moved_q[:, s], z_of[s]) for s in range(NWIN)], axis=0)

    own = jnp.concatenate((own_window, text_q, grad_out_video, grad_out_text), axis=0)
    every = swap(jnp.broadcast_to(own[None], (groups,) + own.shape), PLANE)
    window_rows = (
        every[:, :share].reshape(groups, NWIN, piece, columns).transpose(1, 0, 2, 3)
    ).reshape(-1, columns)
    text_rows = every[:, share : 2 * share].reshape(-1, columns)
    cotangent = jnp.concatenate(
        (
            every[:, 2 * share : 3 * share].reshape(-1, columns),
            every[:, 3 * share :].reshape(-1, columns),
        ),
        axis=0,
    )
    operands = (window_rows, text_rows, cotangent, moved_k, moved_v, text_k, text_v)

    stats = attention_stats(operands, gains, heads)
    pair = lax.psum(stats, "c").reshape(-1, 128)
    chips = lax.axis_size(CHIPS)
    stats = jnp.sum(swap(jnp.broadcast_to(pair[None], (chips,) + pair.shape), CHIPS), axis=0)
    stats = stats.reshape(heads, 2, -1)

    rows, dkey, dvalue, key_text, value_text = attention_grads(
        operands, gains, stats, heads, groups
    )
    returned = swap(
        jnp.concatenate(
            (dkey.reshape(z_size, own_rows, columns), dvalue.reshape(z_size, own_rows, columns)),
            axis=1,
        ),
        "z",
    )
    grad_video_k = returned[:, :own_rows].transpose(1, 0, 2).reshape(own_rows, model)
    grad_video_v = returned[:, own_rows:].transpose(1, 0, 2).reshape(own_rows, model)

    total = jnp.sum(swap(rows, PLANE).astype(F32), axis=0)
    place = lax.axis_index(PLANE)
    own_raw = lax.dynamic_slice_in_dim(window_rows, place * share, share, 0)

    def query_grad(raw, gain, cot):
        shape = (raw.shape[0], heads, HD)
        return pullback(raw.reshape(shape), gain, cot.reshape(shape)).reshape(raw.shape)

    return (
        total[:share].astype(BF16),
        total[share : 2 * share].astype(BF16),
        query_grad(own_raw, gain_video_q, total[2 * share : 3 * share]).astype(BF16),
        query_grad(text_q, gain_text_q, total[3 * share :]).astype(BF16),
        grad_video_k,
        grad_video_v,
        key_text,
        value_text,
    )


def solution(mesh):
    fine = Mesh(mesh.devices.reshape(4, 2, 2, 8, 2), ("y", "xh", "c", "z", "xl"))
    tokens = P(("y", "xh", "c", "z", "xl"), None)
    text = P(PLANE, "z")
    return jax.shard_map(
        local,
        mesh=fine,
        in_specs=(tokens,) * 3 + (text,) * 3 + (P(),) * 5 + (text,) * 2,
        out_specs=(text,) * 4 + (tokens,) * 2 + (text,) * 2,
        check_vma=False,
    )
```

```python
import math

import jax
import jax.numpy as jnp
from jax import lax
from jax.experimental import pallas as pl
from jax.experimental.pallas import tpu as pltpu
from jax.sharding import Mesh, PartitionSpec as P

NWIN = 4
HD = 128
EPS = 1e-06
INV_ROOT = 1.0 / math.sqrt(HD)
LOG2E = math.log2(math.e)
PLANE = ("y", "xh", "c", "xl")
CHIPS = ("y", "xh", "xl")
ROW = ("xh", "xl")
KEY_BLOCK = 256
NT = (((1,), (1,)), ((), ()))
NN = (((1,), (0,)), ((), ()))
TN = (((0,), (0,)), ((), ()))
F32 = jnp.float32
BF16 = jnp.bfloat16


def mm(a, b, dims):
    return lax.dot_general(a, b, dims, preferred_element_type=F32)


def inverse_rms(rows):
    return lax.rsqrt(jnp.mean(rows * rows, axis=-1, keepdims=True) + EPS)


def normed(raw, gain):
    rows = raw.astype(F32)
    return (rows * inverse_rms(rows) * gain).astype(BF16)


def pullback(raw, gain, cot):
    rows = raw.astype(F32)
    inverse = inverse_rms(rows)
    scaled = cot * gain
    along = jnp.mean(rows * scaled, axis=-1, keepdims=True)
    return inverse * (scaled - rows * (inverse * inverse * along))


def normed_queries(win_ref, text_ref, gains_ref):
    return jnp.concatenate(
        (normed(win_ref[...], gains_ref[0:1]), normed(text_ref[...], gains_ref[2:3])), axis=0
    )


def key_parts(k_ref, v_ref, tk_ref, tv_ref, gains_ref):
    parts = []
    step = KEY_BLOCK // k_ref.shape[1]
    for start in range(0, k_ref.shape[0], step):
        spots = slice(start, start + step)
        key = k_ref[spots].reshape(KEY_BLOCK, HD)
        value = v_ref[spots].reshape(KEY_BLOCK, HD)
        parts.append((key, value, gains_ref[1:2], spots))
    parts.append((tk_ref[...], tv_ref[...], gains_ref[3:4], None))
    return parts


def stats_kernel(win_ref, tq_ref, cot_ref, k_ref, v_ref, tk_ref, tv_ref, gains_ref, out_ref):
    queries = normed_queries(win_ref, tq_ref, gains_ref)
    cot = cot_ref[...]
    den = jnp.zeros((1, queries.shape[0]), F32)
    mixed = jnp.zeros((1, queries.shape[0]), F32)
    for raw_key, value, gain, _ in key_parts(k_ref, v_ref, tk_ref, tv_ref, gains_ref):
        key = normed(raw_key, gain)
        weights = jnp.exp2(mm(key, queries, NT) * (INV_ROOT * LOG2E))
        dprobs = mm(value, cot, NT)
        den += jnp.sum(weights, axis=0, keepdims=True)
        mixed += jnp.sum(weights * dprobs, axis=0, keepdims=True)
    out_ref[0, 0:1] = den
    out_ref[0, 1:2] = mixed


def grads_kernel(
    win_ref, tq_ref, cot_ref, k_ref, v_ref, tk_ref, tv_ref, gains_ref, stats_ref,
    rows_ref, dkv_ref, dtk_ref, dtv_ref,
):
    queries = normed_queries(win_ref, tq_ref, gains_ref)
    cot = cot_ref[...]
    count = queries.shape[0]
    inv_den = 1.0 / stats_ref[0, 0:1]
    delta = stats_ref[0, 1:2] * inv_den
    out_t = jnp.zeros((HD, count), F32)
    dq_t = jnp.zeros((HD, count), F32)
    for raw_key, value, gain, spots in key_parts(k_ref, v_ref, tk_ref, tv_ref, gains_ref):
        key = normed(raw_key, gain)
        probs = jnp.exp2(mm(key, queries, NT) * (INV_ROOT * LOG2E)) * inv_den
        probs_16 = probs.astype(BF16)
        dvalue = mm(probs_16, cot, NN).astype(BF16)
        out_t += mm(value, probs_16, TN)
        dscores = (probs * (mm(value, cot, NT) - delta)).astype(BF16)
        dkey = pullback(raw_key, gain, mm(dscores, queries, NN) * INV_ROOT).astype(BF16)
        dq_t += mm(key, dscores, TN)
        if spots is None:
            dtk_ref[...] = dkey
            dtv_ref[...] = dvalue
        else:
            own = dkv_ref.shape[1] // 2
            dkv_ref[spots, :own] = dkey.reshape(-1, own, HD)
            dkv_ref[spots, own:] = dvalue.reshape(-1, own, HD)
    half = count // 2
    outs = out_t.T.astype(BF16)
    dqs = (dq_t * INV_ROOT).T.astype(BF16)
    groups, part = rows_ref.shape[0], rows_ref.shape[1] // 4
    for place, block in enumerate((outs[:half], outs[half:], dqs[:half], dqs[half:])):
        rows_ref[:, place * part : (place + 1) * part] = block.reshape(groups, part, HD)


def column_spec(array):
    lead = array.shape[:-1]
    return pl.BlockSpec(lead + (HD,), lambda head: (0,) * len(lead) + (head,))


def whole_spec(array):
    return pl.BlockSpec(array.shape, lambda head: (0,) * array.ndim)


PARAMS = pltpu.CompilerParams(vmem_limit_bytes=48 * 1024 * 1024)


def attention_stats(operands, gains, heads):
    count = operands[2].shape[0]
    keys = operands[3].shape[0] * operands[3].shape[1]
    return pl.pallas_call(
        stats_kernel,
        grid=(heads,),
        in_specs=[column_spec(a) for a in operands] + [whole_spec(gains)],
        out_specs=pl.BlockSpec((1, 2, count), lambda head: (head, 0, 0)),
        out_shape=jax.ShapeDtypeStruct((heads, 2, count), F32),
        compiler_params=PARAMS,
        cost_estimate=pl.CostEstimate(
            flops=4 * count * keys * heads * HD, bytes_accessed=6000000,
            transcendentals=count * keys * heads,
        ),
    )(*operands, gains)


def attention_grads(operands, gains, stats, heads, groups):
    count = operands[2].shape[0]
    keys = operands[3].shape[0] * operands[3].shape[1]
    text = operands[5].shape[0]
    part = count // groups * 2
    z_size = operands[3].shape[0]
    width = heads * HD
    shapes = [
        jax.ShapeDtypeStruct((groups, part, width), BF16),
        jax.ShapeDtypeStruct((z_size, 2 * operands[3].shape[1], width), BF16),
        jax.ShapeDtypeStruct((text, width), BF16),
        jax.ShapeDtypeStruct((text, width), BF16),
    ]
    return pl.pallas_call(
        grads_kernel,
        grid=(heads,),
        in_specs=[column_spec(a) for a in operands]
        + [whole_spec(gains), pl.BlockSpec((1, 2, count), lambda head: (head, 0, 0))],
        out_specs=[column_spec(s) for s in shapes],
        out_shape=shapes,
        compiler_params=PARAMS,
        cost_estimate=pl.CostEstimate(
            flops=12 * count * keys * heads * HD, bytes_accessed=9000000,
            transcendentals=count * keys * heads,
        ),
    )(*operands, gains, stats)


def swap(array, axes):
    return lax.all_to_all(array, axes, split_axis=0, concat_axis=0, tiled=True)


def push(array, axes, step):
    size = lax.axis_size(axes)
    return lax.ppermute(array, axes, [(i, (i + step) % size) for i in range(size)])


def place(array, index):
    return lax.dynamic_index_in_dim(array, index, 0, keepdims=False, allow_negative_indices=False)


def put(array, part, index):
    return lax.dynamic_update_index_in_dim(array, part, index, 0, allow_negative_indices=False)


def tie(*arrays):
    return lax.optimization_barrier(arrays)


def gather_stage(own, axes):
    size, here = lax.axis_size(axes), lax.axis_index(axes)
    whole = put(jnp.zeros((size,) + own.shape, own.dtype), own, here)
    for step in range(1, size):
        whole = put(whole, push(own, axes, step), (here - step) & (size - 1))
    return whole


def gather_plane(own):
    whole = gather_stage(gather_stage(gather_stage(own, "y"), ROW), "c")
    return whole.reshape((-1,) + own.shape)


def scatter_stage(pieces, axes):
    size, here = lax.axis_size(axes), lax.axis_index(axes)
    return [place(pieces, here)] + [
        push(place(pieces, (here + step) & (size - 1)), axes, step) for step in range(1, size)
    ]


def sum_stage(pieces, axes):
    return sum(piece.astype(F32) for piece in scatter_stage(pieces, axes))


def reduce_plane(pieces):
    shape = pieces.shape[1:]
    pieces = pieces.reshape((lax.axis_size("c"), lax.axis_size(ROW), lax.axis_size("y")) + shape)
    pieces = sum_stage(pieces, "c").astype(BF16)
    pieces = sum_stage(pieces, ROW).astype(BF16)
    return sum_stage(pieces, "y")


def split_heads(rows, groups):
    count = rows.shape[0]
    return rows.reshape(count, groups, -1).transpose(1, 0, 2)


def scatter_window(video_q, window):
    y_size, xl_size, z_size = lax.axis_size("y"), lax.axis_size("xl"), lax.axis_size("z")
    row, model = video_q.shape[0] // lax.axis_size(PLANE), video_q.shape[1]
    rest = window >> (xl_size.bit_length() - 1)
    z_of = rest & (z_size - 1)
    plane_of = (rest >> (z_size.bit_length() - 1)) * xl_size + (window & (xl_size - 1))
    pieces = video_q.reshape(-1, y_size, row, model).transpose(1, 0, 2, 3)
    pieces = swap(pieces.reshape(-1, row, model), PLANE)
    rows = jnp.concatenate([place(pieces, plane_of[slot]) for slot in range(NWIN)], axis=0)
    return split_heads(rows, z_size), z_of


def pick_window(came, z_of):
    row = came.shape[1] // NWIN
    rows = jnp.stack(
        [place(came, z_of[s])[s * row : (s + 1) * row] for s in range(NWIN)]
    )
    rows = gather_stage(rows, "y")
    return rows.transpose(1, 0, 2, 3).reshape(NWIN, row * lax.axis_size("y"), -1)


def local(
    video_q, video_k, video_v, text_q, text_k, text_v,
    gain_video_q, gain_video_k, gain_text_q, gain_text_k,
    window, grad_out_video, grad_out_text,
):
    z_size = lax.axis_size("z")
    groups = lax.axis_size(PLANE)
    own_rows, model = video_q.shape
    columns = model // z_size
    heads = columns // HD
    share = grad_out_video.shape[0]
    gains = jnp.stack((gain_video_q, gain_video_k, gain_text_q, gain_text_k))

    text = jnp.stack((text_q, grad_out_video, grad_out_text))
    every = gather_plane(text)
    picked, z_of = scatter_window(video_q, window)
    sent = jnp.concatenate((split_heads(video_k, z_size), picked), axis=1)
    moved = swap(sent, "z")
    rows = pick_window(moved[:, own_rows:], z_of)
    own_window = place(rows, lax.axis_index("y"))
    sent_v, moved = tie(split_heads(video_v, z_size), moved)
    moved_v = swap(sent_v, "z")
    moved_k = moved[:, :own_rows]
    window_rows = gather_stage(gather_stage(rows, ROW), "c").reshape(-1, columns)
    text_rows = every[:, 0].reshape(-1, columns)
    cotangent = jnp.concatenate(
        (every[:, 1].reshape(-1, columns), every[:, 2].reshape(-1, columns)), axis=0
    )
    operands = (window_rows, text_rows, cotangent, moved_k, moved_v, text_k, text_v)

    stats = attention_stats(operands, gains, heads)
    pair = lax.psum(stats, "c").reshape(-1, 128)
    chips = lax.axis_size(CHIPS)
    stats = jnp.sum(swap(jnp.broadcast_to(pair[None], (chips,) + pair.shape), CHIPS), axis=0)
    stats = stats.reshape(heads, 2, -1)

    rows, dmoved, key_text, value_text = attention_grads(operands, gains, stats, heads, groups)
    returned = swap(dmoved, "z")
    grad_video_k = returned[:, :own_rows].transpose(1, 0, 2).reshape(own_rows, model)
    grad_video_v = returned[:, own_rows:].transpose(1, 0, 2).reshape(own_rows, model)

    total = reduce_plane(rows)

    def query_grad(raw, gain, cot):
        shape = (raw.shape[0], heads, HD)
        return pullback(raw.reshape(shape), gain, cot.reshape(shape)).reshape(raw.shape)

    return (
        total[:share].astype(BF16),
        total[share : 2 * share].astype(BF16),
        query_grad(own_window, gain_video_q, total[2 * share : 3 * share]).astype(BF16),
        query_grad(text_q, gain_text_q, total[3 * share :]).astype(BF16),
        grad_video_k,
        grad_video_v,
        key_text,
        value_text,
    )


def solution(mesh):
    fine = Mesh(mesh.devices.reshape(4, 2, 2, 8, 2), ("y", "xh", "c", "z", "xl"))
    tokens = P(("y", "xh", "c", "z", "xl"), None)
    text = P(PLANE, "z")
    return jax.shard_map(
        local,
        mesh=fine,
        in_specs=(tokens,) * 3 + (text,) * 3 + (P(),) * 5 + (text,) * 2,
        out_specs=(text,) * 4 + (tokens,) * 2 + (text,) * 2,
        check_vma=False,
    )
```

```python
import math

import jax
import jax.numpy as jnp
from jax import lax
from jax.experimental import pallas as pl
from jax.experimental.pallas import tpu as pltpu
from jax.sharding import Mesh, PartitionSpec as P

NWIN = 4
HD = 128
EPS = 1e-06
INV_ROOT = 1.0 / math.sqrt(HD)
LOG2E = math.log2(math.e)
PLANE = ("y", "xh", "c", "xl")
FLAT = ("xh", "c", "xl")
ROW = ("xh", "xl")
KEY_BLOCK = 256
NT = (((1,), (1,)), ((), ()))
NN = (((1,), (0,)), ((), ()))
TN = (((0,), (0,)), ((), ()))
F32 = jnp.float32
BF16 = jnp.bfloat16


def mm(a, b, dims):
    return lax.dot_general(a, b, dims, preferred_element_type=F32)


def inverse_rms(rows):
    return lax.rsqrt(jnp.mean(rows * rows, axis=-1, keepdims=True) + EPS)


def normed(raw, gain):
    rows = raw.astype(F32)
    return (rows * inverse_rms(rows) * gain).astype(BF16)


def pullback(raw, gain, cot):
    rows = raw.astype(F32)
    inverse = inverse_rms(rows)
    scaled = cot * gain
    along = jnp.mean(rows * scaled, axis=-1, keepdims=True)
    return inverse * (scaled - rows * (inverse * inverse * along))


def normed_queries(win_ref, text_ref, gains_ref):
    return jnp.concatenate(
        (normed(win_ref[...], gains_ref[0:1]), normed(text_ref[...], gains_ref[2:3])), axis=0
    )


def key_parts(k_ref, v_ref, tk_ref, tv_ref, gains_ref):
    parts = []
    step = KEY_BLOCK // v_ref.shape[1]
    for start in range(0, v_ref.shape[0], step):
        spots = slice(start, start + step)
        key = k_ref[spots].reshape(KEY_BLOCK, HD)
        value = v_ref[spots].reshape(KEY_BLOCK, HD)
        parts.append((key, value, gains_ref[1:2], spots))
    parts.append((tk_ref[...], tv_ref[...], gains_ref[3:4], None))
    return parts


def stats_kernel(win_ref, tq_ref, cot_ref, k_ref, v_ref, tk_ref, tv_ref, gains_ref, out_ref):
    queries = normed_queries(win_ref, tq_ref, gains_ref)
    cot = cot_ref[...]
    den = jnp.zeros((1, queries.shape[0]), F32)
    mixed = jnp.zeros((1, queries.shape[0]), F32)
    for raw_key, value, gain, _ in key_parts(k_ref, v_ref, tk_ref, tv_ref, gains_ref):
        key = normed(raw_key, gain)
        weights = jnp.exp2(mm(key, queries, NT) * (INV_ROOT * LOG2E))
        dprobs = mm(value, cot, NT)
        den += jnp.sum(weights, axis=0, keepdims=True)
        mixed += jnp.sum(weights * dprobs, axis=0, keepdims=True)
    out_ref[0, 0:1] = den
    out_ref[0, 1:2] = mixed


def grads_kernel(
    win_ref, tq_ref, cot_ref, k_ref, v_ref, tk_ref, tv_ref, gains_ref, stats_ref,
    rows_ref, dkv_ref, dtk_ref, dtv_ref,
):
    queries = normed_queries(win_ref, tq_ref, gains_ref)
    cot = cot_ref[...]
    count = queries.shape[0]
    inv_den = 1.0 / stats_ref[0, 0:1]
    delta = stats_ref[0, 1:2] * inv_den
    out_t = jnp.zeros((HD, count), F32)
    dq_t = jnp.zeros((HD, count), F32)
    for raw_key, value, gain, spots in key_parts(k_ref, v_ref, tk_ref, tv_ref, gains_ref):
        key = normed(raw_key, gain)
        probs = jnp.exp2(mm(key, queries, NT) * (INV_ROOT * LOG2E)) * inv_den
        probs_16 = probs.astype(BF16)
        dvalue = mm(probs_16, cot, NN).astype(BF16)
        out_t += mm(value, probs_16, TN)
        dscores = (probs * (mm(value, cot, NT) - delta)).astype(BF16)
        dkey = pullback(raw_key, gain, mm(dscores, queries, NN) * INV_ROOT).astype(BF16)
        dq_t += mm(key, dscores, TN)
        if spots is None:
            dtk_ref[...] = dkey
            dtv_ref[...] = dvalue
        else:
            own = dkv_ref.shape[1] // 2
            dkv_ref[spots, :own] = dkey.reshape(-1, own, HD)
            dkv_ref[spots, own:] = dvalue.reshape(-1, own, HD)
    half = count // 2
    outs = out_t.T.astype(BF16)
    dqs = (dq_t * INV_ROOT).T.astype(BF16)
    groups, part = rows_ref.shape[0], rows_ref.shape[1] // 4
    for place, block in enumerate((outs[:half], outs[half:], dqs[:half], dqs[half:])):
        rows_ref[:, place * part : (place + 1) * part] = block.reshape(groups, part, HD)


def column_spec(shape):
    lead = tuple(shape[:-1])
    return pl.BlockSpec(lead + (HD,), lambda head: (0,) * len(lead) + (head,))


PARAMS = pltpu.CompilerParams(vmem_limit_bytes=48 * 1024 * 1024)


def operand_specs(operands, gains):
    win, text, cot, moved_k, moved_v, text_k, text_v = operands
    shapes = [win.shape, text.shape, cot.shape, moved_v.shape, moved_v.shape]
    specs = [column_spec(shape) for shape in shapes + [text_k.shape, text_v.shape]]
    return specs + [pl.BlockSpec(gains.shape, lambda head: (0, 0))]


def cost(operands, heads, dots):
    work = operands[2].shape[0] * operands[4].shape[0] * operands[4].shape[1] * heads
    return pl.CostEstimate(
        flops=2 * dots * work * HD, bytes_accessed=2000000 * heads, transcendentals=work
    )


def attention_stats(operands, gains, heads):
    count = operands[2].shape[0]
    return pl.pallas_call(
        stats_kernel,
        grid=(heads,),
        in_specs=operand_specs(operands, gains),
        out_specs=pl.BlockSpec((1, 2, count), lambda head: (head, 0, 0)),
        out_shape=jax.ShapeDtypeStruct((heads, 2, count), F32),
        compiler_params=PARAMS,
        cost_estimate=cost(operands, heads, 2),
    )(*operands, gains)


def attention_grads(operands, gains, stats, heads, groups):
    count = operands[2].shape[0]
    z_size, own = operands[4].shape[:2]
    text = operands[5].shape[0]
    width = heads * HD
    shapes = [
        jax.ShapeDtypeStruct((groups, count // groups * 2, width), BF16),
        jax.ShapeDtypeStruct((z_size, 2 * own, width), BF16),
        jax.ShapeDtypeStruct((text, width), BF16),
        jax.ShapeDtypeStruct((text, width), BF16),
    ]
    return pl.pallas_call(
        grads_kernel,
        grid=(heads,),
        in_specs=operand_specs(operands, gains)
        + [pl.BlockSpec((1, 2, count), lambda head: (head, 0, 0))],
        out_specs=[column_spec(s.shape) for s in shapes],
        out_shape=shapes,
        compiler_params=PARAMS,
        cost_estimate=cost(operands, heads, 6),
    )(*operands, gains, stats)


def swap(array, axes):
    return lax.all_to_all(array, axes, split_axis=0, concat_axis=0, tiled=True)


def push(array, axes, step):
    if step == 0:
        return array
    size = lax.axis_size(axes)
    return lax.ppermute(array, axes, [(i, (i + step) % size) for i in range(size)])


def place(array, index):
    return lax.dynamic_index_in_dim(array, index, 0, keepdims=False, allow_negative_indices=False)


def put(array, part, index):
    return lax.dynamic_update_index_in_dim(array, part, index, 0, allow_negative_indices=False)


def tie(*arrays):
    return lax.optimization_barrier(arrays)


def gather_stage(own, axes):
    size, here = lax.axis_size(axes), lax.axis_index(axes)
    whole = put(jnp.zeros((size,) + own.shape, own.dtype), own, here)
    for step in range(1, size):
        whole = put(whole, push(own, axes, step), (here - step) & (size - 1))
    return whole


def gather_plane(own):
    whole = gather_stage(gather_stage(gather_stage(own, "y"), ROW), "c")
    return whole.reshape((-1,) + own.shape)


def scatter_stage(pieces, axes):
    size, here = lax.axis_size(axes), lax.axis_index(axes)
    return [place(pieces, here)] + [
        push(place(pieces, (here + step) & (size - 1)), axes, step) for step in range(1, size)
    ]


def sum_stage(pieces, axes):
    return sum(piece.astype(F32) for piece in scatter_stage(pieces, axes))


def reduce_row(pieces):
    shape = pieces.shape[1:]
    pieces = pieces.reshape((lax.axis_size("c"), lax.axis_size(ROW), lax.axis_size("y")) + shape)
    pieces = sum_stage(pieces, "c").astype(BF16)
    return sum_stage(pieces, ROW).astype(BF16)


def sum_plane(part):
    for axes in ("c", ROW, "y"):
        size = lax.axis_size(axes)
        bit = 1
        while bit < size:
            part = part + lax.ppermute(part, axes, [(i, i ^ bit) for i in range(size)])
            bit *= 2
    return part


def pack_kernel(flat_ref, pieces_ref, k_ref, out_ref):
    own, rows = k_ref.shape[0], pieces_ref.shape[1]
    out_ref[0, :own] = k_ref[...]
    for slot in range(NWIN):
        start = own + slot * rows
        out_ref[0, start : start + rows] = pieces_ref[flat_ref[slot]]


def pack(flat_of, pieces, video_k, z_size):
    count, rows, model = pieces.shape
    own = video_k.shape[0]
    columns = model // z_size
    total = own + NWIN * rows
    return pl.pallas_call(
        pack_kernel,
        grid_spec=pltpu.PrefetchScalarGridSpec(
            num_scalar_prefetch=1,
            grid=(z_size,),
            in_specs=[
                pl.BlockSpec((count, rows, columns), lambda z, _: (0, 0, z)),
                pl.BlockSpec((own, columns), lambda z, _: (0, z)),
            ],
            out_specs=pl.BlockSpec((1, total, columns), lambda z, _: (z, 0, 0)),
        ),
        out_shape=jax.ShapeDtypeStruct((z_size, total, columns), BF16),
    )(flat_of, pieces, video_k)


def unpack_kernel(_, came_ref, out_ref):
    out_ref[...] = came_ref[...]


def unpack(z_of, came, own, rows):
    columns = came.shape[2]
    first = own // rows
    return pl.pallas_call(
        unpack_kernel,
        grid_spec=pltpu.PrefetchScalarGridSpec(
            num_scalar_prefetch=1,
            grid=(NWIN,),
            in_specs=[
                pl.BlockSpec((1, rows, columns), lambda s, z_ref: (z_ref[s], first + s, 0))
            ],
            out_specs=pl.BlockSpec((1, rows, columns), lambda s, _: (s, 0, 0)),
        ),
        out_shape=jax.ShapeDtypeStruct((NWIN, rows, columns), BF16),
    )(z_of, came)


def choose_kernel(info_ref, *refs):
    parts, (out_ref, own_ref) = refs[:-2], refs[-2:]
    for slot in range(NWIN):
        source = info_ref[slot]
        for index, part in enumerate(parts):

            @pl.when(source == index)
            def _():
                out_ref[slot] = part[slot]

    own_ref[...] = out_ref[info_ref[NWIN]]


def choose(info, parts):
    shape = parts[0].shape
    whole = pl.BlockSpec(memory_space=pltpu.VMEM)
    return pl.pallas_call(
        choose_kernel,
        in_specs=[pl.BlockSpec(memory_space=pltpu.SMEM)] + [whole] * len(parts),
        out_specs=[whole, whole],
        out_shape=[
            jax.ShapeDtypeStruct(shape, BF16), jax.ShapeDtypeStruct(shape[1:], BF16)
        ],
    )(info, *parts)


def merge_kernel(came_ref, k_ref, v_ref):
    own = k_ref.shape[0]
    k_ref[...] = came_ref[0, :own]
    v_ref[...] = came_ref[0, own:]


def merge(came):
    z_size, rows, width = came.shape
    out = pl.BlockSpec((rows // 2, width), lambda z: (0, z))
    return pl.pallas_call(
        merge_kernel,
        grid=(z_size,),
        in_specs=[pl.BlockSpec((1, rows, width), lambda z: (z, 0, 0))],
        out_specs=[out, out],
        out_shape=[jax.ShapeDtypeStruct((rows // 2, z_size * width), BF16)] * 2,
    )(came)


def local(
    video_q, video_k, video_v, text_q, text_k, text_v,
    gain_video_q, gain_video_k, gain_text_q, gain_text_k,
    window, grad_out_video, grad_out_text,
):
    z_size, xl_size = lax.axis_size("z"), lax.axis_size("xl")
    flat_size, y_size = lax.axis_size(FLAT), lax.axis_size("y")
    groups = lax.axis_size(PLANE)
    own_rows, model = video_q.shape
    columns = model // z_size
    heads = columns // HD
    share = grad_out_video.shape[0]
    gains = jnp.stack((gain_video_q, gain_video_k, gain_text_q, gain_text_k))
    y = lax.axis_index("y")

    rest = window >> (xl_size.bit_length() - 1)
    z_of = rest & (z_size - 1)
    rest = rest >> (z_size.bit_length() - 1)
    flat_of = (rest & (flat_size // xl_size - 1)) * xl_size + (window & (xl_size - 1))
    from_y = (y - (rest >> ((flat_size // xl_size).bit_length() - 1))) & (y_size - 1)

    pieces = swap(video_q.reshape(flat_size, -1, model), FLAT)
    rows = pieces.shape[1]
    moved_k = swap(pack(flat_of, pieces, video_k, z_size), "z")

    text = jnp.stack((text_q, grad_out_video, grad_out_text))
    text, pieces = tie(text, pieces)
    text = gather_stage(gather_stage(text, "y"), ROW)
    own = unpack(z_of, moved_k, own_rows, rows)
    video_v, moved_k = tie(video_v, moved_k)
    sent = video_v.reshape(own_rows, z_size, columns).transpose(1, 0, 2)
    moved_v = swap(sent, "z")

    own, own_window = choose(
        jnp.concatenate((from_y, y[None])), [push(own, "y", step) for step in range(y_size)]
    )
    own = gather_stage(own, ROW)
    own, moved_v = tie(own, moved_v)
    text = text.transpose(2, 0, 1, 3, 4)
    halves = gather_stage(jnp.concatenate((own[None], text.reshape((-1,) + own.shape)), 0), "c")
    window_rows, text_rows, *cotangent = (
        halves[:, kind].reshape(-1, columns) for kind in range(4)
    )
    cotangent = jnp.concatenate(cotangent, axis=0)
    operands = (window_rows, text_rows, cotangent, moved_k, moved_v, text_k, text_v)

    stats = sum_plane(attention_stats(operands, gains, heads))
    out, dmoved, key_text, value_text = attention_grads(operands, gains, stats, heads, groups)
    back = swap(dmoved, "z")
    total = sum_stage(reduce_row(out), "y")
    grad_video_k, grad_video_v = merge(back)

    def query_grad(raw, gain, cot):
        shape = (raw.shape[0], heads, HD)
        return pullback(raw.reshape(shape), gain, cot.reshape(shape)).reshape(raw.shape)

    return (
        total[:share].astype(BF16),
        total[share : 2 * share].astype(BF16),
        query_grad(own_window, gain_video_q, total[2 * share : 3 * share]).astype(BF16),
        query_grad(text_q, gain_text_q, total[3 * share :]).astype(BF16),
        grad_video_k,
        grad_video_v,
        key_text,
        value_text,
    )


def solution(mesh):
    fine = Mesh(mesh.devices.reshape(4, 2, 2, 8, 2), ("y", "xh", "c", "z", "xl"))
    tokens = P(("y", "xh", "c", "z", "xl"), None)
    text = P(PLANE, "z")
    return jax.shard_map(
        local,
        mesh=fine,
        in_specs=(tokens,) * 3 + (text,) * 3 + (P(),) * 5 + (text,) * 2,
        out_specs=(text,) * 4 + (tokens,) * 2 + (text,) * 2,
        check_vma=False,
    )
```

```python
import math

import jax
import jax.numpy as jnp
from jax import lax
from jax.experimental import pallas as pl
from jax.experimental.pallas import tpu as pltpu
from jax.sharding import Mesh, PartitionSpec as P

NWIN = 4
HD = 128
EPS = 1e-06
INV_ROOT = 1.0 / math.sqrt(HD)
LOG2E = math.log2(math.e)
PLANE = ("y", "xh", "c", "xl")
ROW = ("xh", "xl")
KEY_BLOCK = 256
VMEM = 48 * 1024 * 1024
NT = (((1,), (1,)), ((), ()))
NN = (((1,), (0,)), ((), ()))
TN = (((0,), (0,)), ((), ()))
F32 = jnp.float32
BF16 = jnp.bfloat16


def mm(a, b, dims):
    return lax.dot_general(a, b, dims, preferred_element_type=F32)


def inverse_rms(rows):
    return lax.rsqrt(jnp.mean(rows * rows, axis=-1, keepdims=True) + EPS)


def normed(raw, gain):
    rows = raw.astype(F32)
    return (rows * inverse_rms(rows) * gain).astype(BF16)


def pullback(raw, gain, cot):
    rows = raw.astype(F32)
    inverse = inverse_rms(rows)
    scaled = cot * gain
    along = jnp.mean(rows * scaled, axis=-1, keepdims=True)
    return inverse * (scaled - rows * (inverse * inverse * along))


def normed_queries(win_ref, text_ref, gains_ref):
    return jnp.concatenate(
        (normed(win_ref[...], gains_ref[0:1]), normed(text_ref[...], gains_ref[2:3])), axis=0
    )


def key_parts(k_ref, v_ref, tk_ref, tv_ref, gains_ref):
    parts = []
    step = KEY_BLOCK // v_ref.shape[1]
    for start in range(0, v_ref.shape[0], step):
        spots = slice(start, start + step)
        key = k_ref[spots].reshape(KEY_BLOCK, HD)
        value = v_ref[spots].reshape(KEY_BLOCK, HD)
        parts.append((key, value, gains_ref[1:2], spots))
    parts.append((tk_ref[...], tv_ref[...], gains_ref[3:4], None))
    return parts


def stats_kernel(win_ref, tq_ref, cot_ref, k_ref, v_ref, tk_ref, tv_ref, gains_ref, out_ref):
    queries = normed_queries(win_ref, tq_ref, gains_ref)
    cot = cot_ref[...]
    den = jnp.zeros((1, queries.shape[0]), F32)
    mixed = jnp.zeros((1, queries.shape[0]), F32)
    for raw_key, value, gain, _ in key_parts(k_ref, v_ref, tk_ref, tv_ref, gains_ref):
        key = normed(raw_key, gain)
        weights = jnp.exp2(mm(key, queries, NT) * (INV_ROOT * LOG2E))
        dprobs = mm(value, cot, NT)
        den += jnp.sum(weights, axis=0, keepdims=True)
        mixed += jnp.sum(weights * dprobs, axis=0, keepdims=True)
    out_ref[0, 0:1] = den
    out_ref[0, 1:2] = mixed


def grads_kernel(
    win_ref, tq_ref, cot_ref, k_ref, v_ref, tk_ref, tv_ref, gains_ref, stats_ref,
    rows_ref, dkv_ref, dtk_ref, dtv_ref,
):
    queries = normed_queries(win_ref, tq_ref, gains_ref)
    cot = cot_ref[...]
    count = queries.shape[0]
    inv_den = 1.0 / stats_ref[0, 0:1]
    delta = stats_ref[0, 1:2] * inv_den
    out_t = jnp.zeros((HD, count), F32)
    dq_t = jnp.zeros((HD, count), F32)
    for raw_key, value, gain, spots in key_parts(k_ref, v_ref, tk_ref, tv_ref, gains_ref):
        key = normed(raw_key, gain)
        probs = jnp.exp2(mm(key, queries, NT) * (INV_ROOT * LOG2E)) * inv_den
        probs_16 = probs.astype(BF16)
        dvalue = mm(probs_16, cot, NN).astype(BF16)
        out_t += mm(value, probs_16, TN)
        dscores = (probs * (mm(value, cot, NT) - delta)).astype(BF16)
        dkey = pullback(raw_key, gain, mm(dscores, queries, NN) * INV_ROOT).astype(BF16)
        dq_t += mm(key, dscores, TN)
        if spots is None:
            dtk_ref[...] = dkey
            dtv_ref[...] = dvalue
        else:
            own = dkv_ref.shape[1] // 2
            dkv_ref[spots, :own] = dkey.reshape(-1, own, HD)
            dkv_ref[spots, own:] = dvalue.reshape(-1, own, HD)
    half = count // 2
    outs = out_t.T.astype(BF16)
    dqs = (dq_t * INV_ROOT).T.astype(BF16)
    groups, part = rows_ref.shape[0], rows_ref.shape[1] // 4
    for place, block in enumerate((outs[:half], outs[half:], dqs[:half], dqs[half:])):
        rows_ref[:, place * part : (place + 1) * part] = block.reshape(groups, part, HD)


def column_spec(shape):
    lead = tuple(shape[:-1])
    return pl.BlockSpec(lead + (HD,), lambda head: (0,) * len(lead) + (head,))


PARAMS = pltpu.CompilerParams(vmem_limit_bytes=VMEM)


def operand_specs(operands, gains):
    win, text, cot, moved_k, moved_v, text_k, text_v = operands
    shapes = [win.shape, text.shape, cot.shape, moved_v.shape, moved_v.shape]
    specs = [column_spec(shape) for shape in shapes + [text_k.shape, text_v.shape]]
    return specs + [pl.BlockSpec(gains.shape, lambda head: (0, 0))]


def cost(operands, heads, dots):
    work = operands[2].shape[0] * operands[4].shape[0] * operands[4].shape[1] * heads
    return pl.CostEstimate(
        flops=2 * dots * work * HD, bytes_accessed=2000000 * heads, transcendentals=work
    )


def attention_stats(operands, gains, heads):
    count = operands[2].shape[0]
    return pl.pallas_call(
        stats_kernel,
        grid=(heads,),
        in_specs=operand_specs(operands, gains),
        out_specs=pl.BlockSpec((1, 2, count), lambda head: (head, 0, 0)),
        out_shape=jax.ShapeDtypeStruct((heads, 2, count), F32),
        compiler_params=PARAMS,
        cost_estimate=cost(operands, heads, 2),
    )(*operands, gains)


def attention_grads(operands, gains, stats, heads, groups):
    count = operands[2].shape[0]
    z_size, own = operands[4].shape[:2]
    text = operands[5].shape[0]
    width = heads * HD
    shapes = [
        jax.ShapeDtypeStruct((groups, count // groups * 2, width), BF16),
        jax.ShapeDtypeStruct((z_size, 2 * own, width), BF16),
        jax.ShapeDtypeStruct((text, width), BF16),
        jax.ShapeDtypeStruct((text, width), BF16),
    ]
    return pl.pallas_call(
        grads_kernel,
        grid=(heads,),
        in_specs=operand_specs(operands, gains)
        + [pl.BlockSpec((1, 2, count), lambda head: (head, 0, 0))],
        out_specs=[column_spec(s.shape) for s in shapes],
        out_shape=shapes,
        compiler_params=PARAMS,
        cost_estimate=cost(operands, heads, 6),
    )(*operands, gains, stats)


def swap(array, axes):
    return lax.all_to_all(array, axes, split_axis=0, concat_axis=0, tiled=True)


def push(array, axes, step):
    if step == 0:
        return array
    size = lax.axis_size(axes)
    return lax.ppermute(array, axes, [(i, (i + step) % size) for i in range(size)])


def place(array, index):
    return lax.dynamic_index_in_dim(array, index, 0, keepdims=False, allow_negative_indices=False)


def put(array, part, index):
    return lax.dynamic_update_index_in_dim(array, part, index, 0, allow_negative_indices=False)


def tie(*arrays):
    return lax.optimization_barrier(arrays)


def gather_stage(own, axes):
    size, here = lax.axis_size(axes), lax.axis_index(axes)
    whole = put(jnp.zeros((size,) + own.shape, own.dtype), own, here)
    for step in range(1, size):
        whole = put(whole, push(own, axes, step), (here - step) & (size - 1))
    return whole


def gather_plane(own):
    whole = gather_stage(gather_stage(gather_stage(own, "y"), ROW), "c")
    return whole.reshape((-1,) + own.shape)


def scatter_stage(pieces, axes):
    size, here = lax.axis_size(axes), lax.axis_index(axes)
    return [place(pieces, here)] + [
        push(place(pieces, (here + step) & (size - 1)), axes, step) for step in range(1, size)
    ]


def sum_stage(pieces, axes):
    return sum(piece.astype(F32) for piece in scatter_stage(pieces, axes))


def reduce_row(pieces):
    shape = pieces.shape[1:]
    pieces = pieces.reshape((lax.axis_size("c"), lax.axis_size(ROW), lax.axis_size("y")) + shape)
    pieces = sum_stage(pieces, "c").astype(BF16)
    return sum_stage(pieces, ROW).astype(BF16)


def sum_plane(part):
    for axes in ("c", ROW, "y"):
        size = lax.axis_size(axes)
        bit = 1
        while bit < size:
            part = part + lax.ppermute(part, axes, [(i, i ^ bit) for i in range(size)])
            bit *= 2
    return part


def fetch_window(video_q, window):
    y, x, c = (lax.axis_index(axes) for axes in ("y", ROW, "c"))
    xl_size, z_size = lax.axis_size("xl"), lax.axis_size("z")
    y_size, x_size, c_size = lax.axis_size("y"), lax.axis_size(ROW), lax.axis_size("c")
    xh_size = x_size // xl_size
    model = video_q.shape[1]

    block = lax.dynamic_slice_in_dim(
        jnp.concatenate((window, window)), y, NWIN, 0, allow_negative_indices=False
    )
    xl_of = block & (xl_size - 1)
    rest = block >> (xl_size.bit_length() - 1)
    z_of = rest & (z_size - 1)
    rest = rest >> (z_size.bit_length() - 1)
    c_of = rest & (c_size - 1)
    rest = rest >> (c_size.bit_length() - 1)
    xh_of = rest & (xh_size - 1)
    y_of = rest >> (xh_size.bit_length() - 1)
    from_x = (x - xh_of * xl_size - xl_of) & (x_size - 1)
    source = from_x * c_size + ((c - c_of) & (c_size - 1))
    from_y = (y - y_of[0]) & (y_size - 1)

    pieces = video_q.reshape(xh_size, c_size, xl_size, -1, model).transpose(1, 0, 2, 3, 4)
    pieces = pieces.reshape(c_size, x_size, -1, model)
    pieces = jnp.stack(scatter_stage(pieces, "c"), axis=1)
    pieces = jnp.concatenate(scatter_stage(pieces, ROW), axis=0)
    came = [place(pieces, source[0])] + [
        push(place(pieces, source[step]), "y", step) for step in range(1, y_size)
    ]
    return place(jnp.stack(came), from_y), z_of[0]


def split_heads(rows, groups):
    count = rows.shape[0]
    return rows.reshape(count, groups, -1).transpose(1, 0, 2)


def merge_kernel(came_ref, k_ref, v_ref, sems):
    own = k_ref.shape[0]
    z_size, _, width = came_ref.shape
    copies = []
    for z in range(z_size):
        for part, ref in enumerate((k_ref, v_ref)):
            copies.append(
                pltpu.make_async_copy(
                    came_ref.at[z, pl.ds(part * own, own)],
                    ref.at[:, pl.ds(z * width, width)],
                    sems.at[z, part],
                )
            )
    for copy in copies:
        copy.start()
    for copy in copies:
        copy.wait()


def merge(came):
    z_size, rows, width = came.shape
    anywhere = pl.BlockSpec(memory_space=pl.ANY)
    return pl.pallas_call(
        merge_kernel,
        in_specs=[pl.BlockSpec(memory_space=pltpu.VMEM)],
        out_specs=[anywhere, anywhere],
        out_shape=[jax.ShapeDtypeStruct((rows // 2, z_size * width), BF16)] * 2,
        scratch_shapes=[pltpu.SemaphoreType.DMA((z_size, 2))],
    )(came)


def local(
    video_q, video_k, video_v, text_q, text_k, text_v,
    gain_video_q, gain_video_k, gain_text_q, gain_text_k,
    window, grad_out_video, grad_out_text,
):
    z_size = lax.axis_size("z")
    groups = lax.axis_size(PLANE)
    own_rows, model = video_q.shape
    columns = model // z_size
    heads = columns // HD
    share = grad_out_video.shape[0]
    gains = jnp.stack((gain_video_q, gain_video_k, gain_text_q, gain_text_k))

    moved_k = swap(split_heads(video_k, z_size), "z")
    picked, z_of = fetch_window(video_q, window)
    picked, moved_k = tie(picked, moved_k)
    came = swap(split_heads(picked, z_size), "z")
    own_window = place(came, z_of)
    sent_v, own_window = tie(split_heads(video_v, z_size), own_window)
    moved_v = swap(sent_v, "z")
    own = jnp.stack((own_window, text_q, grad_out_video, grad_out_text))
    own = gather_stage(gather_stage(own, "y"), ROW)
    own, moved_v = tie(own, moved_v)
    own = gather_stage(own.transpose(2, 0, 1, 3, 4), "c")
    window_rows, text_rows, *cotangent = (own[:, kind].reshape(-1, columns) for kind in range(4))
    cotangent = jnp.concatenate(cotangent, axis=0)
    operands = (window_rows, text_rows, cotangent, moved_k, moved_v, text_k, text_v)

    stats = sum_plane(attention_stats(operands, gains, heads))
    out, dmoved, key_text, value_text = attention_grads(operands, gains, stats, heads, groups)
    back = swap(dmoved, "z")
    total = sum_stage(reduce_row(out), "y")
    grad_video_k, grad_video_v = merge(back)

    def query_grad(raw, gain, cot):
        shape = (raw.shape[0], heads, HD)
        return pullback(raw.reshape(shape), gain, cot.reshape(shape)).reshape(raw.shape)

    return (
        total[:share].astype(BF16),
        total[share : 2 * share].astype(BF16),
        query_grad(own_window, gain_video_q, total[2 * share : 3 * share]).astype(BF16),
        query_grad(text_q, gain_text_q, total[3 * share :]).astype(BF16),
        grad_video_k,
        grad_video_v,
        key_text,
        value_text,
    )


def solution(mesh):
    fine = Mesh(mesh.devices.reshape(4, 2, 2, 8, 2), ("y", "xh", "c", "z", "xl"))
    tokens = P(("y", "xh", "c", "z", "xl"), None)
    text = P(PLANE, "z")
    return jax.shard_map(
        local,
        mesh=fine,
        in_specs=(tokens,) * 3 + (text,) * 3 + (P(),) * 5 + (text,) * 2,
        out_specs=(text,) * 4 + (tokens,) * 2 + (text,) * 2,
        check_vma=False,
    )
```

```python
import math

import jax
import jax.numpy as jnp
from jax import lax
from jax.experimental import pallas as pl
from jax.experimental.pallas import tpu as pltpu
from jax.sharding import Mesh, PartitionSpec as P

NWIN = 4
HD = 128
EPS = 1e-06
INV_ROOT = 1.0 / math.sqrt(HD)
LOG2E = math.log2(math.e)
PLANE = ("y", "xh", "c", "xl")
ROW = ("xh", "xl")
KEY_BLOCK = 256
VMEM = 48 * 1024 * 1024
NT = (((1,), (1,)), ((), ()))
NN = (((1,), (0,)), ((), ()))
TN = (((0,), (0,)), ((), ()))
F32 = jnp.float32
BF16 = jnp.bfloat16


def mm(a, b, dims):
    return lax.dot_general(a, b, dims, preferred_element_type=F32)


def inverse_rms(rows):
    return lax.rsqrt(jnp.mean(rows * rows, axis=-1, keepdims=True) + EPS)


def normed(raw, gain):
    rows = raw.astype(F32)
    return (rows * inverse_rms(rows) * gain).astype(BF16)


def pullback(raw, gain, cot):
    rows = raw.astype(F32)
    inverse = inverse_rms(rows)
    scaled = cot * gain
    along = jnp.mean(rows * scaled, axis=-1, keepdims=True)
    return inverse * (scaled - rows * (inverse * inverse * along))


def normed_queries(win_ref, text_ref, gains_ref):
    return jnp.concatenate(
        (normed(win_ref[...], gains_ref[0:1]), normed(text_ref[...], gains_ref[2:3])), axis=0
    )


def key_parts(k_ref, v_ref, tk_ref, tv_ref, gains_ref):
    parts = []
    step = KEY_BLOCK // v_ref.shape[1]
    for start in range(0, v_ref.shape[0], step):
        spots = slice(start, start + step)
        key = k_ref[spots].reshape(KEY_BLOCK, HD)
        value = v_ref[spots].reshape(KEY_BLOCK, HD)
        parts.append((key, value, gains_ref[1:2], spots))
    parts.append((tk_ref[...], tv_ref[...], gains_ref[3:4], None))
    return parts


def stats_kernel(win_ref, tq_ref, cot_ref, k_ref, v_ref, tk_ref, tv_ref, gains_ref, out_ref):
    queries = normed_queries(win_ref, tq_ref, gains_ref)
    cot = cot_ref[...]
    den = jnp.zeros((1, queries.shape[0]), F32)
    mixed = jnp.zeros((1, queries.shape[0]), F32)
    for raw_key, value, gain, _ in key_parts(k_ref, v_ref, tk_ref, tv_ref, gains_ref):
        key = normed(raw_key, gain)
        weights = jnp.exp2(mm(key, queries, NT) * (INV_ROOT * LOG2E))
        dprobs = mm(value, cot, NT)
        den += jnp.sum(weights, axis=0, keepdims=True)
        mixed += jnp.sum(weights * dprobs, axis=0, keepdims=True)
    out_ref[0, 0:1] = den
    out_ref[0, 1:2] = mixed


def grads_kernel(
    win_ref, tq_ref, cot_ref, k_ref, v_ref, tk_ref, tv_ref, gains_ref, stats_ref,
    rows_ref, dkv_ref, dtk_ref, dtv_ref,
):
    queries = normed_queries(win_ref, tq_ref, gains_ref)
    cot = cot_ref[...]
    count = queries.shape[0]
    inv_den = 1.0 / stats_ref[0, 0:1]
    delta = stats_ref[0, 1:2] * inv_den
    out_t = jnp.zeros((HD, count), F32)
    dq_t = jnp.zeros((HD, count), F32)
    for raw_key, value, gain, spots in key_parts(k_ref, v_ref, tk_ref, tv_ref, gains_ref):
        key = normed(raw_key, gain)
        probs = jnp.exp2(mm(key, queries, NT) * (INV_ROOT * LOG2E)) * inv_den
        probs_16 = probs.astype(BF16)
        dvalue = mm(probs_16, cot, NN).astype(BF16)
        out_t += mm(value, probs_16, TN)
        dscores = (probs * (mm(value, cot, NT) - delta)).astype(BF16)
        dkey = pullback(raw_key, gain, mm(dscores, queries, NN) * INV_ROOT).astype(BF16)
        dq_t += mm(key, dscores, TN)
        if spots is None:
            dtk_ref[...] = dkey
            dtv_ref[...] = dvalue
        else:
            own = dkv_ref.shape[1] // 2
            dkv_ref[spots, :own] = dkey.reshape(-1, own, HD)
            dkv_ref[spots, own:] = dvalue.reshape(-1, own, HD)
    half = count // 2
    outs = out_t.T.astype(BF16)
    dqs = (dq_t * INV_ROOT).T.astype(BF16)
    groups, part = rows_ref.shape[0], rows_ref.shape[1] // 4
    for place, block in enumerate((outs[:half], outs[half:], dqs[:half], dqs[half:])):
        rows_ref[:, place * part : (place + 1) * part] = block.reshape(groups, part, HD)


def column_spec(shape, first=0):
    lead = tuple(shape[:-1])
    return pl.BlockSpec(lead + (HD,), lambda head: (0,) * len(lead) + (head + first,))


PARAMS = pltpu.CompilerParams(vmem_limit_bytes=VMEM)


def operand_specs(operands, gains, first):
    specs = [column_spec(array.shape, first) for array in operands]
    return specs + [pl.BlockSpec(gains.shape, lambda head: (0, 0))]


def cost(operands, heads, dots):
    _, _, cot, moved_k, moved_v, *_ = operands
    keys = moved_k.shape[0] * (moved_k.shape[1] + moved_v.shape[1]) // 2
    work = cot.shape[0] * keys * heads
    return pl.CostEstimate(
        flops=2 * dots * work * HD, bytes_accessed=2000000 * heads, transcendentals=work
    )


def attention_stats(operands, gains, heads):
    count = operands[2].shape[0]
    return pl.pallas_call(
        stats_kernel,
        grid=(heads,),
        in_specs=operand_specs(operands, gains, 0),
        out_specs=pl.BlockSpec((1, 2, count), lambda head: (head, 0, 0)),
        out_shape=jax.ShapeDtypeStruct((heads, 2, count), F32),
        compiler_params=PARAMS,
        cost_estimate=cost(operands, heads, 2),
    )(*operands, gains)


def attention_grads(operands, gains, stats, first, last, groups):
    _, _, cot, moved_k, moved_v, text_k, _ = operands
    count, heads = cot.shape[0], last - first
    width = heads * HD
    shapes = [
        jax.ShapeDtypeStruct((groups, count // groups * 2, width), BF16),
        jax.ShapeDtypeStruct(
            (moved_k.shape[0], moved_k.shape[1] + moved_v.shape[1], width), BF16
        ),
        jax.ShapeDtypeStruct((text_k.shape[0], width), BF16),
        jax.ShapeDtypeStruct((text_k.shape[0], width), BF16),
    ]
    return pl.pallas_call(
        grads_kernel,
        grid=(heads,),
        in_specs=operand_specs(operands, gains, first)
        + [pl.BlockSpec((1, 2, count), lambda head: (head + first, 0, 0))],
        out_specs=[column_spec(s.shape) for s in shapes],
        out_shape=shapes,
        compiler_params=PARAMS,
        cost_estimate=cost(operands, heads, 6),
    )(*operands, gains, stats)


def swap(array, axes):
    return lax.all_to_all(array, axes, split_axis=0, concat_axis=0, tiled=True)


def push(array, axes, step):
    if step == 0:
        return array
    size = lax.axis_size(axes)
    return lax.ppermute(array, axes, [(i, (i + step) % size) for i in range(size)])


def place(array, index):
    return lax.dynamic_index_in_dim(array, index, 0, keepdims=False, allow_negative_indices=False)


def put(array, part, index):
    return lax.dynamic_update_index_in_dim(array, part, index, 0, allow_negative_indices=False)


def tie(*arrays):
    return lax.optimization_barrier(arrays)


def gather_stage(own, axes):
    size, here = lax.axis_size(axes), lax.axis_index(axes)
    whole = put(jnp.zeros((size,) + own.shape, own.dtype), own, here)
    for step in range(1, size):
        whole = put(whole, push(own, axes, step), (here - step) & (size - 1))
    return whole


def gather_plane(own):
    whole = gather_stage(gather_stage(gather_stage(own, "y"), ROW), "c")
    return whole.reshape((-1,) + own.shape)


def scatter_stage(pieces, axes):
    size, here = lax.axis_size(axes), lax.axis_index(axes)
    return [place(pieces, here)] + [
        push(place(pieces, (here + step) & (size - 1)), axes, step) for step in range(1, size)
    ]


def sum_stage(pieces, axes):
    return sum(piece.astype(F32) for piece in scatter_stage(pieces, axes))


def reduce_row(pieces):
    shape = pieces.shape[1:]
    pieces = pieces.reshape((lax.axis_size("c"), lax.axis_size(ROW), lax.axis_size("y")) + shape)
    pieces = sum_stage(pieces, "c").astype(BF16)
    return sum_stage(pieces, ROW).astype(BF16)


def sum_plane(part):
    for axes in ("c", ROW, "y"):
        part = sum(push(part, axes, step) for step in range(lax.axis_size(axes)))
    return part


def choose_kernel(source_ref, *refs):
    parts, outs = refs[:-NWIN], refs[-NWIN:]
    count = parts[0].shape[0]
    for step, out in enumerate(outs):
        source = source_ref[step]
        for index in range(len(parts) * count):

            @pl.when(source == index)
            def _():
                out[...] = parts[index // count][index % count]


def choose(source, parts):
    whole = pl.BlockSpec(memory_space=pltpu.VMEM)
    return pl.pallas_call(
        choose_kernel,
        in_specs=[pl.BlockSpec(memory_space=pltpu.SMEM)] + [whole] * len(parts),
        out_specs=[whole] * NWIN,
        out_shape=[jax.ShapeDtypeStruct(parts[0].shape[1:], BF16)] * NWIN,
    )(source, *parts)


def fetch_window(video_q, window):
    y, x, c = (lax.axis_index(axes) for axes in ("y", ROW, "c"))
    xl_size, z_size = lax.axis_size("xl"), lax.axis_size("z")
    y_size, x_size, c_size = lax.axis_size("y"), lax.axis_size(ROW), lax.axis_size("c")
    xh_size = x_size // xl_size
    model = video_q.shape[1]

    block = lax.dynamic_slice_in_dim(
        jnp.concatenate((window, window)), y, NWIN, 0, allow_negative_indices=False
    )
    xl_of = block & (xl_size - 1)
    rest = block >> (xl_size.bit_length() - 1)
    z_of = rest & (z_size - 1)
    rest = rest >> (z_size.bit_length() - 1)
    c_of = rest & (c_size - 1)
    rest = rest >> (c_size.bit_length() - 1)
    xh_of = rest & (xh_size - 1)
    y_of = rest >> (xh_size.bit_length() - 1)
    from_x = (x - xh_of * xl_size - xl_of) & (x_size - 1)
    source = from_x * c_size + ((c - c_of) & (c_size - 1))
    from_y = (y - y_of[0]) & (y_size - 1)

    pieces = video_q.reshape(xh_size, c_size, xl_size, -1, model)

    def side(index):
        part = lax.dynamic_index_in_dim(pieces, index, 1, False, allow_negative_indices=False)
        return part.reshape(x_size, -1, model)

    pieces = jnp.stack((side(c), push(side(c ^ 1), "c", 1)), axis=1)
    chosen = choose(source, scatter_stage(pieces, ROW))
    came = [chosen[0]] + [push(chosen[step], "y", step) for step in range(1, y_size)]
    return place(jnp.stack(came), from_y), z_of[0]


def split_heads(rows, groups):
    count = rows.shape[0]
    return rows.reshape(count, groups, -1).transpose(1, 0, 2)


def merge_kernel(lead_ref, late_ref, k_ref, v_ref, sems):
    own = k_ref.shape[0]
    z_size, _, first = lead_ref.shape
    width = first + late_ref.shape[2]
    copies = []
    for z in range(z_size):
        for part, ref in enumerate((k_ref, v_ref)):
            for half, (source, start) in enumerate(((lead_ref, 0), (late_ref, first))):
                copies.append(
                    pltpu.make_async_copy(
                        source.at[z, pl.ds(part * own, own)],
                        ref.at[:, pl.ds(z * width + start, source.shape[2])],
                        sems.at[z, part, half],
                    )
                )
    for copy in copies:
        copy.start()
    for copy in copies:
        copy.wait()


def merge(lead, late):
    z_size, rows, first = lead.shape
    width = first + late.shape[2]
    anywhere = pl.BlockSpec(memory_space=pl.ANY)
    return pl.pallas_call(
        merge_kernel,
        in_specs=[pl.BlockSpec(memory_space=pltpu.VMEM)] * 2,
        out_specs=[anywhere, anywhere],
        out_shape=[jax.ShapeDtypeStruct((rows // 2, z_size * width), BF16)] * 2,
        scratch_shapes=[pltpu.SemaphoreType.DMA((z_size, 2, 2))],
    )(lead, late)


def local(
    video_q, video_k, video_v, text_q, text_k, text_v,
    gain_video_q, gain_video_k, gain_text_q, gain_text_k,
    window, grad_out_video, grad_out_text,
):
    z_size = lax.axis_size("z")
    groups = lax.axis_size(PLANE)
    own_rows, model = video_q.shape
    columns = model // z_size
    heads = columns // HD
    share = grad_out_video.shape[0]
    gains = jnp.stack((gain_video_q, gain_video_k, gain_text_q, gain_text_k))

    moved_k = swap(split_heads(video_k, z_size), "z")
    picked, z_of = fetch_window(video_q, window)
    picked, moved_k = tie(picked, moved_k)
    came = swap(split_heads(picked, z_size), "z")
    own_window = place(came, z_of)
    sent_v, own_window = tie(split_heads(video_v, z_size), own_window)
    moved_v = swap(sent_v, "z")
    own = jnp.stack((own_window, text_q, grad_out_video, grad_out_text))
    own = gather_stage(gather_stage(own, "y"), ROW)
    text = gather_stage(own[:, :, 1:].transpose(2, 0, 1, 3, 4), "c")
    own, moved_v = tie(own[:, :, 0], moved_v)
    window_rows = gather_stage(own, "c").reshape(-1, columns)
    text_rows, *cotangent = (text[:, kind].reshape(-1, columns) for kind in range(3))
    cotangent = jnp.concatenate(cotangent, axis=0)
    operands = (window_rows, text_rows, cotangent, moved_k, moved_v, text_k, text_v)

    stats = sum_plane(attention_stats(operands, gains, heads))
    outs, backs, *dtext = zip(
        *(
            attention_grads(operands, gains, stats, first, last, groups)
            for first, last in ((0, 1), (1, heads))
        )
    )
    backs = [swap(back, "z") for back in backs]
    out, backs[0] = tie(jnp.concatenate(outs, axis=2), backs[0])
    total = sum_stage(reduce_row(out), "y")
    grad_video_k, grad_video_v = merge(*backs)
    key_text, value_text = (jnp.concatenate(parts, axis=1) for parts in dtext)

    def query_grad(raw, gain, cot):
        shape = (raw.shape[0], heads, HD)
        return pullback(raw.reshape(shape), gain, cot.reshape(shape)).reshape(raw.shape)

    return (
        total[:share].astype(BF16),
        total[share : 2 * share].astype(BF16),
        query_grad(own_window, gain_video_q, total[2 * share : 3 * share]).astype(BF16),
        query_grad(text_q, gain_text_q, total[3 * share :]).astype(BF16),
        grad_video_k,
        grad_video_v,
        key_text,
        value_text,
    )


def solution(mesh):
    fine = Mesh(mesh.devices.reshape(4, 2, 2, 8, 2), ("y", "xh", "c", "z", "xl"))
    tokens = P(("y", "xh", "c", "z", "xl"), None)
    text = P(PLANE, "z")
    return jax.shard_map(
        local,
        mesh=fine,
        in_specs=(tokens,) * 3 + (text,) * 3 + (P(),) * 5 + (text,) * 2,
        out_specs=(text,) * 4 + (tokens,) * 2 + (text,) * 2,
        check_vma=False,
    )
```

```python
import math

import jax
import jax.numpy as jnp
from jax import lax
from jax.experimental import pallas as pl
from jax.experimental.pallas import tpu as pltpu
from jax.sharding import Mesh, PartitionSpec as P

NWIN = 4
HD = 128
EPS = 1e-06
INV_ROOT = 1.0 / math.sqrt(HD)
LOG2E = math.log2(math.e)
PLANE = ("y", "xh", "c", "xl")
ROW = ("xh", "xl")
KEY_BLOCK = 1024
EARLY = 48
VMEM = 48 * 1024 * 1024
NT = (((1,), (1,)), ((), ()))
NN = (((1,), (0,)), ((), ()))
TN = (((0,), (0,)), ((), ()))
F32 = jnp.float32
BF16 = jnp.bfloat16


def mm(a, b, dims):
    return lax.dot_general(a, b, dims, preferred_element_type=F32)


def inverse_rms(rows):
    return lax.rsqrt(jnp.mean(rows * rows, axis=-1, keepdims=True) + EPS)


def normed(raw, gain):
    rows = raw.astype(F32)
    return (rows * inverse_rms(rows) * gain).astype(BF16)


def pullback(raw, gain, cot):
    rows = raw.astype(F32)
    inverse = inverse_rms(rows)
    scaled = cot * gain
    along = jnp.mean(rows * scaled, axis=-1, keepdims=True)
    return inverse * (scaled - rows * (inverse * inverse * along))


def normed_queries(win_ref, text_ref, gains_ref):
    return jnp.concatenate(
        (normed(win_ref[...], gains_ref[0:1]), normed(text_ref[...], gains_ref[2:3])), axis=0
    )


def key_parts(k_ref, v_ref, tk_ref, tv_ref, gains_ref):
    parts = []
    own = (k_ref.shape[1] + v_ref.shape[1]) // 2
    step = KEY_BLOCK // own
    for start in range(0, v_ref.shape[0], step):
        spots = slice(start, start + step)
        key = k_ref[spots, :own].reshape(KEY_BLOCK, HD)
        value = jnp.concatenate((k_ref[spots, own:], v_ref[spots]), axis=1)
        value = value.reshape(KEY_BLOCK, HD)
        parts.append((key, value, gains_ref[1:2], spots))
    parts.append((tk_ref[...], tv_ref[...], gains_ref[3:4], None))
    return parts


def stats_kernel(win_ref, tq_ref, cot_ref, k_ref, v_ref, tk_ref, tv_ref, gains_ref, out_ref):
    queries = normed_queries(win_ref, tq_ref, gains_ref)
    cot = cot_ref[...]
    den = jnp.zeros((1, queries.shape[0]), F32)
    mixed = jnp.zeros((1, queries.shape[0]), F32)
    for raw_key, value, gain, _ in key_parts(k_ref, v_ref, tk_ref, tv_ref, gains_ref):
        key = normed(raw_key, gain)
        weights = jnp.exp2(mm(key, queries, NT) * (INV_ROOT * LOG2E))
        dprobs = mm(value, cot, NT)
        den += jnp.sum(weights, axis=0, keepdims=True)
        mixed += jnp.sum(weights * dprobs, axis=0, keepdims=True)
    out_ref[0, 0:1] = den
    out_ref[0, 1:2] = mixed


def grads_kernel(
    win_ref, tq_ref, cot_ref, k_ref, v_ref, tk_ref, tv_ref, gains_ref, stats_ref,
    rows_ref, dkv_ref, dtk_ref, dtv_ref,
):
    queries = normed_queries(win_ref, tq_ref, gains_ref)
    cot = cot_ref[...]
    count = queries.shape[0]
    inv_den = 1.0 / stats_ref[0, 0:1]
    delta = stats_ref[0, 1:2] * inv_den
    out_t = jnp.zeros((HD, count), F32)
    dq_t = jnp.zeros((HD, count), F32)
    for raw_key, value, gain, spots in key_parts(k_ref, v_ref, tk_ref, tv_ref, gains_ref):
        key = normed(raw_key, gain)
        probs = jnp.exp2(mm(key, queries, NT) * (INV_ROOT * LOG2E)) * inv_den
        probs_16 = probs.astype(BF16)
        dvalue = mm(probs_16, cot, NN).astype(BF16)
        out_t += mm(value, probs_16, TN)
        dscores = (probs * (mm(value, cot, NT) - delta)).astype(BF16)
        dkey = pullback(raw_key, gain, mm(dscores, queries, NN) * INV_ROOT).astype(BF16)
        dq_t += mm(key, dscores, TN)
        if spots is None:
            dtk_ref[...] = dkey
            dtv_ref[...] = dvalue
        else:
            own = dkv_ref.shape[1] // 2
            dkv_ref[spots, :own] = dkey.reshape(-1, own, HD)
            dkv_ref[spots, own:] = dvalue.reshape(-1, own, HD)
    half = count // 2
    outs = out_t.T.astype(BF16)
    dqs = (dq_t * INV_ROOT).T.astype(BF16)
    groups, part = rows_ref.shape[0], rows_ref.shape[1] // 4
    for place, block in enumerate((outs[:half], outs[half:], dqs[:half], dqs[half:])):
        rows_ref[:, place * part : (place + 1) * part] = block.reshape(groups, part, HD)


def column_spec(shape):
    lead = tuple(shape[:-1])
    return pl.BlockSpec(lead + (HD,), lambda head: (0,) * len(lead) + (head,))


PARAMS = pltpu.CompilerParams(vmem_limit_bytes=VMEM)


def operand_specs(operands, gains):
    specs = [column_spec(array.shape) for array in operands]
    return specs + [pl.BlockSpec(gains.shape, lambda head: (0, 0))]


def cost(operands, heads, dots):
    _, _, cot, moved_k, moved_v, *_ = operands
    keys = moved_k.shape[0] * (moved_k.shape[1] + moved_v.shape[1]) // 2
    work = cot.shape[0] * keys * heads
    return pl.CostEstimate(
        flops=2 * dots * work * HD, bytes_accessed=2000000 * heads, transcendentals=work
    )


def attention_stats(operands, gains, heads):
    count = operands[2].shape[0]
    return pl.pallas_call(
        stats_kernel,
        grid=(heads,),
        in_specs=operand_specs(operands, gains),
        out_specs=pl.BlockSpec((1, 2, count), lambda head: (head, 0, 0)),
        out_shape=jax.ShapeDtypeStruct((heads, 2, count), F32),
        compiler_params=PARAMS,
        cost_estimate=cost(operands, heads, 2),
    )(*operands, gains)


def attention_grads(operands, gains, stats, heads, groups):
    _, _, cot, moved_k, moved_v, text_k, _ = operands
    count = cot.shape[0]
    width = heads * HD
    shapes = [
        jax.ShapeDtypeStruct((groups, count // groups * 2, width), BF16),
        jax.ShapeDtypeStruct(
            (moved_k.shape[0], moved_k.shape[1] + moved_v.shape[1], width), BF16
        ),
        jax.ShapeDtypeStruct((text_k.shape[0], width), BF16),
        jax.ShapeDtypeStruct((text_k.shape[0], width), BF16),
    ]
    return pl.pallas_call(
        grads_kernel,
        grid=(heads,),
        in_specs=operand_specs(operands, gains)
        + [pl.BlockSpec((1, 2, count), lambda head: (head, 0, 0))],
        out_specs=[column_spec(s.shape) for s in shapes],
        out_shape=shapes,
        compiler_params=PARAMS,
        cost_estimate=cost(operands, heads, 6),
    )(*operands, gains, stats)


def swap(array, axes):
    return lax.all_to_all(array, axes, split_axis=0, concat_axis=0, tiled=True)


def push(array, axes, step):
    if step == 0:
        return array
    size = lax.axis_size(axes)
    return lax.ppermute(array, axes, [(i, (i + step) % size) for i in range(size)])


def place(array, index):
    return lax.dynamic_index_in_dim(array, index, 0, keepdims=False, allow_negative_indices=False)


def put(array, part, index):
    return lax.dynamic_update_index_in_dim(array, part, index, 0, allow_negative_indices=False)


def tie(*arrays):
    return lax.optimization_barrier(arrays)


def gather_stage(own, axes):
    size, here = lax.axis_size(axes), lax.axis_index(axes)
    whole = put(jnp.zeros((size,) + own.shape, own.dtype), own, here)
    for step in range(1, size):
        whole = put(whole, push(own, axes, step), (here - step) & (size - 1))
    return whole


def gather_plane(own):
    whole = gather_stage(gather_stage(gather_stage(own, "y"), ROW), "c")
    return whole.reshape((-1,) + own.shape)


def scatter_stage(pieces, axes):
    size, here = lax.axis_size(axes), lax.axis_index(axes)
    return [place(pieces, here)] + [
        push(place(pieces, (here + step) & (size - 1)), axes, step) for step in range(1, size)
    ]


def sum_stage(pieces, axes):
    return sum(piece.astype(F32) for piece in scatter_stage(pieces, axes))


def reduce_row(pieces):
    shape = pieces.shape[1:]
    pieces = pieces.reshape((lax.axis_size("c"), lax.axis_size(ROW), lax.axis_size("y")) + shape)
    pieces = sum_stage(pieces, "c").astype(BF16)
    return sum_stage(pieces, ROW).astype(BF16)


def sum_plane(part):
    for axes in ("c", ROW, "y"):
        part = sum(push(part, axes, step) for step in range(lax.axis_size(axes)))
    return part


def choose_kernel(source_ref, *refs):
    parts, outs = refs[:-NWIN], refs[-NWIN:]
    count = parts[0].shape[0]
    for step, out in enumerate(outs):
        source = source_ref[step]
        for index in range(len(parts) * count):

            @pl.when(source == index)
            def _():
                out[...] = parts[index // count][index % count]


def choose(source, parts):
    whole = pl.BlockSpec(memory_space=pltpu.VMEM)
    return pl.pallas_call(
        choose_kernel,
        in_specs=[pl.BlockSpec(memory_space=pltpu.SMEM)] + [whole] * len(parts),
        out_specs=[whole] * NWIN,
        out_shape=[jax.ShapeDtypeStruct(parts[0].shape[1:], BF16)] * NWIN,
    )(source, *parts)


def fetch_window(video_q, window):
    y, x, c = (lax.axis_index(axes) for axes in ("y", ROW, "c"))
    xl_size, z_size = lax.axis_size("xl"), lax.axis_size("z")
    y_size, x_size, c_size = lax.axis_size("y"), lax.axis_size(ROW), lax.axis_size("c")
    xh_size = x_size // xl_size
    model = video_q.shape[1]

    block = lax.dynamic_slice_in_dim(
        jnp.concatenate((window, window)), y, NWIN, 0, allow_negative_indices=False
    )
    xl_of = block & (xl_size - 1)
    rest = block >> (xl_size.bit_length() - 1)
    z_of = rest & (z_size - 1)
    rest = rest >> (z_size.bit_length() - 1)
    c_of = rest & (c_size - 1)
    rest = rest >> (c_size.bit_length() - 1)
    xh_of = rest & (xh_size - 1)
    y_of = rest >> (xh_size.bit_length() - 1)
    from_x = (x - xh_of * xl_size - xl_of) & (x_size - 1)
    source = from_x * c_size + ((c - c_of) & (c_size - 1))
    from_y = (y - y_of[0]) & (y_size - 1)

    pieces = video_q.reshape(xh_size, c_size, xl_size, -1, model)

    def side(index):
        part = lax.dynamic_index_in_dim(pieces, index, 1, False, allow_negative_indices=False)
        return part.reshape(x_size, -1, model)

    pieces = jnp.stack((side(c), push(side(c ^ 1), "c", 1)), axis=1)
    chosen = choose(source, scatter_stage(pieces, ROW))
    came = [chosen[0]] + [push(chosen[step], "y", step) for step in range(1, y_size)]
    return place(jnp.stack(came), from_y), z_of[0]


def split_heads(rows, groups):
    count = rows.shape[0]
    return rows.reshape(count, groups, -1).transpose(1, 0, 2)


def merge_kernel(came_ref, k_ref, v_ref, sems):
    own = k_ref.shape[0]
    z_size, _, width = came_ref.shape
    copies = []
    for z in range(z_size):
        for part, ref in enumerate((k_ref, v_ref)):
            copies.append(
                pltpu.make_async_copy(
                    came_ref.at[z, pl.ds(part * own, own)],
                    ref.at[:, pl.ds(z * width, width)],
                    sems.at[z, part],
                )
            )
    for copy in copies:
        copy.start()
    for copy in copies:
        copy.wait()


def merge(came):
    z_size, rows, width = came.shape
    anywhere = pl.BlockSpec(memory_space=pl.ANY)
    return pl.pallas_call(
        merge_kernel,
        in_specs=[pl.BlockSpec(memory_space=pltpu.VMEM)],
        out_specs=[anywhere, anywhere],
        out_shape=[jax.ShapeDtypeStruct((rows // 2, z_size * width), BF16)] * 2,
        scratch_shapes=[pltpu.SemaphoreType.DMA((z_size, 2))],
    )(came)


def local(
    video_q, video_k, video_v, text_q, text_k, text_v,
    gain_video_q, gain_video_k, gain_text_q, gain_text_k,
    window, grad_out_video, grad_out_text,
):
    z_size = lax.axis_size("z")
    groups = lax.axis_size(PLANE)
    own_rows, model = video_q.shape
    columns = model // z_size
    heads = columns // HD
    share = grad_out_video.shape[0]
    gains = jnp.stack((gain_video_q, gain_video_k, gain_text_q, gain_text_k))

    first_v, last_v = video_v[:EARLY], video_v[EARLY:]
    moved_k = swap(split_heads(jnp.concatenate((video_k, first_v), axis=0), z_size), "z")
    picked, z_of = fetch_window(video_q, window)
    picked, moved_k = tie(picked, moved_k)
    came = swap(split_heads(picked, z_size), "z")
    own_window = place(came, z_of)
    sent_v, own_window = tie(split_heads(last_v, z_size), own_window)
    moved_v = swap(sent_v, "z")
    own = jnp.stack((own_window, text_q, grad_out_video, grad_out_text))
    own = gather_stage(gather_stage(own, "y"), ROW)
    own, moved_v = tie(own, moved_v)
    own = gather_stage(own.transpose(2, 0, 1, 3, 4), "c")
    window_rows, text_rows, *cotangent = (own[:, kind].reshape(-1, columns) for kind in range(4))
    cotangent = jnp.concatenate(cotangent, axis=0)
    operands = (window_rows, text_rows, cotangent, moved_k, moved_v, text_k, text_v)

    stats = sum_plane(attention_stats(operands, gains, heads))
    out, back, key_text, value_text = attention_grads(operands, gains, stats, heads, groups)
    back = swap(back, "z")
    total = sum_stage(reduce_row(out), "y")
    grad_video_k, grad_video_v = merge(back)

    def query_grad(raw, gain, cot):
        shape = (raw.shape[0], heads, HD)
        return pullback(raw.reshape(shape), gain, cot.reshape(shape)).reshape(raw.shape)

    return (
        total[:share].astype(BF16),
        total[share : 2 * share].astype(BF16),
        query_grad(own_window, gain_video_q, total[2 * share : 3 * share]).astype(BF16),
        query_grad(text_q, gain_text_q, total[3 * share :]).astype(BF16),
        grad_video_k,
        grad_video_v,
        key_text,
        value_text,
    )


def solution(mesh):
    fine = Mesh(mesh.devices.reshape(4, 2, 2, 8, 2), ("y", "xh", "c", "z", "xl"))
    tokens = P(("y", "xh", "c", "z", "xl"), None)
    text = P(PLANE, "z")
    return jax.shard_map(
        local,
        mesh=fine,
        in_specs=(tokens,) * 3 + (text,) * 3 + (P(),) * 5 + (text,) * 2,
        out_specs=(text,) * 4 + (tokens,) * 2 + (text,) * 2,
        check_vma=False,
    )
```

```python
import math

import jax
import jax.numpy as jnp
from jax import lax
from jax.experimental import pallas as pl
from jax.experimental.pallas import tpu as pltpu
from jax.sharding import Mesh, PartitionSpec as P

NWIN = 4
HD = 128
EPS = 1e-06
INV_ROOT = 1.0 / math.sqrt(HD)
LOG2E = math.log2(math.e)
PLANE = ("y", "xh", "c", "xl")
ROW = ("xh", "xl")
KEY_BLOCK = 1024
EARLY = 48
VMEM = 52 * 1024 * 1024
NT = (((1,), (1,)), ((), ()))
NN = (((1,), (0,)), ((), ()))
TN = (((0,), (0,)), ((), ()))
F32 = jnp.float32
BF16 = jnp.bfloat16


def mm(a, b, dims):
    return lax.dot_general(a, b, dims, preferred_element_type=F32)


def inverse_rms(rows):
    return lax.rsqrt(jnp.mean(rows * rows, axis=-1, keepdims=True) + EPS)


def normed(raw, gain):
    rows = raw.astype(F32)
    return (rows * inverse_rms(rows) * gain).astype(BF16)


def pullback(raw, gain, cot):
    rows = raw.astype(F32)
    inverse = inverse_rms(rows)
    scaled = cot * gain
    along = jnp.mean(rows * scaled, axis=-1, keepdims=True)
    return inverse * (scaled - rows * (inverse * inverse * along))


def normed_queries(win_ref, text_ref, gains_ref):
    return jnp.concatenate(
        (normed(win_ref[...], gains_ref[0:1]), normed(text_ref[...], gains_ref[2:3])), axis=0
    )


def key_parts(k_ref, v_ref, tk_ref, tv_ref, gains_ref):
    parts = []
    own = (k_ref.shape[1] + v_ref.shape[1]) // 2
    step = KEY_BLOCK // own
    for start in range(0, v_ref.shape[0], step):
        spots = slice(start, start + step)
        key = k_ref[spots, :own].reshape(KEY_BLOCK, HD)
        value = jnp.concatenate((k_ref[spots, own:], v_ref[spots]), axis=1)
        value = value.reshape(KEY_BLOCK, HD)
        parts.append((key, value, gains_ref[1:2], spots))
    parts.append((tk_ref[...], tv_ref[...], gains_ref[3:4], None))
    return parts


def stats_kernel(win_ref, tq_ref, cot_ref, k_ref, v_ref, tk_ref, tv_ref, gains_ref, out_ref):
    queries = normed_queries(win_ref, tq_ref, gains_ref)
    cot = cot_ref[...]
    den = jnp.zeros((1, queries.shape[0]), F32)
    mixed = jnp.zeros((1, queries.shape[0]), F32)
    for raw_key, value, gain, _ in key_parts(k_ref, v_ref, tk_ref, tv_ref, gains_ref):
        key = normed(raw_key, gain)
        weights = jnp.exp2(mm(key, queries, NT) * (INV_ROOT * LOG2E))
        dprobs = mm(value, cot, NT)
        den += jnp.sum(weights, axis=0, keepdims=True)
        mixed += jnp.sum(weights * dprobs, axis=0, keepdims=True)
    out_ref[0, 0:1] = den
    out_ref[0, 1:2] = mixed


def grads_kernel(
    win_ref, tq_ref, cot_ref, k_ref, v_ref, tk_ref, tv_ref, gains_ref, stats_ref,
    rows_ref, dkv_ref, dtk_ref, dtv_ref,
):
    queries = normed_queries(win_ref, tq_ref, gains_ref)
    cot = cot_ref[...]
    count = queries.shape[0]
    inv_den = 1.0 / stats_ref[0, 0:1]
    delta = stats_ref[0, 1:2] * inv_den
    out_t = jnp.zeros((HD, count), F32)
    dq_t = jnp.zeros((HD, count), F32)
    for raw_key, value, gain, spots in key_parts(k_ref, v_ref, tk_ref, tv_ref, gains_ref):
        key = normed(raw_key, gain)
        probs = jnp.exp2(mm(key, queries, NT) * (INV_ROOT * LOG2E)) * inv_den
        probs_16 = probs.astype(BF16)
        dvalue = mm(probs_16, cot, NN).astype(BF16)
        out_t += mm(value, probs_16, TN)
        dscores = (probs * (mm(value, cot, NT) - delta)).astype(BF16)
        dkey = pullback(raw_key, gain, mm(dscores, queries, NN) * INV_ROOT).astype(BF16)
        dq_t += mm(key, dscores, TN)
        if spots is None:
            dtk_ref[...] = dkey
            dtv_ref[...] = dvalue
        else:
            own = dkv_ref.shape[1] // 2
            dkv_ref[spots, :own] = dkey.reshape(-1, own, HD)
            dkv_ref[spots, own:] = dvalue.reshape(-1, own, HD)
    half = count // 2
    outs = out_t.T.astype(BF16)
    dqs = (dq_t * INV_ROOT).T.astype(BF16)
    groups, part = rows_ref.shape[0], rows_ref.shape[1] // 4
    for place, block in enumerate((outs[:half], outs[half:], dqs[:half], dqs[half:])):
        rows_ref[:, place * part : (place + 1) * part] = block.reshape(groups, part, HD)


def column_spec(shape):
    lead = tuple(shape[:-1])
    return pl.BlockSpec(lead + (HD,), lambda head: (0,) * len(lead) + (head,))


PARAMS = pltpu.CompilerParams(vmem_limit_bytes=VMEM)


def operand_specs(operands, gains):
    specs = [column_spec(array.shape) for array in operands]
    return specs + [pl.BlockSpec(gains.shape, lambda head: (0, 0))]


def cost(operands, heads, dots):
    _, _, cot, moved_k, moved_v, *_ = operands
    keys = moved_k.shape[0] * (moved_k.shape[1] + moved_v.shape[1]) // 2
    work = cot.shape[0] * keys * heads
    return pl.CostEstimate(
        flops=2 * dots * work * HD, bytes_accessed=2000000 * heads, transcendentals=work
    )


def attention_stats(operands, gains, heads):
    count = operands[2].shape[0]
    return pl.pallas_call(
        stats_kernel,
        grid=(heads,),
        in_specs=operand_specs(operands, gains),
        out_specs=pl.BlockSpec((1, 2, count), lambda head: (head, 0, 0)),
        out_shape=jax.ShapeDtypeStruct((heads, 2, count), F32),
        compiler_params=PARAMS,
        cost_estimate=cost(operands, heads, 2),
    )(*operands, gains)


def attention_grads(operands, gains, stats, heads, groups):
    _, _, cot, moved_k, moved_v, text_k, _ = operands
    count = cot.shape[0]
    width = heads * HD
    shapes = [
        jax.ShapeDtypeStruct((groups, count // groups * 2, width), BF16),
        jax.ShapeDtypeStruct(
            (moved_k.shape[0], moved_k.shape[1] + moved_v.shape[1], width), BF16
        ),
        jax.ShapeDtypeStruct((text_k.shape[0], width), BF16),
        jax.ShapeDtypeStruct((text_k.shape[0], width), BF16),
    ]
    return pl.pallas_call(
        grads_kernel,
        grid=(heads,),
        in_specs=operand_specs(operands, gains)
        + [pl.BlockSpec((1, 2, count), lambda head: (head, 0, 0))],
        out_specs=[column_spec(s.shape) for s in shapes],
        out_shape=shapes,
        compiler_params=PARAMS,
        cost_estimate=cost(operands, heads, 6),
    )(*operands, gains, stats)


def swap(array, axes):
    return lax.all_to_all(array, axes, split_axis=0, concat_axis=0, tiled=True)


def push(array, axes, step):
    if step == 0:
        return array
    size = lax.axis_size(axes)
    return lax.ppermute(array, axes, [(i, (i + step) % size) for i in range(size)])


def place(array, index):
    return lax.dynamic_index_in_dim(array, index, 0, keepdims=False, allow_negative_indices=False)


def put(array, part, index):
    return lax.dynamic_update_index_in_dim(array, part, index, 0, allow_negative_indices=False)


def tie(*arrays):
    return lax.optimization_barrier(arrays)


def gather_stage(own, axes):
    size, here = lax.axis_size(axes), lax.axis_index(axes)
    whole = put(jnp.zeros((size,) + own.shape, own.dtype), own, here)
    for step in range(1, size):
        whole = put(whole, push(own, axes, step), (here - step) & (size - 1))
    return whole


def gather_plane(own):
    whole = gather_stage(gather_stage(gather_stage(own, "y"), ROW), "c")
    return whole.reshape((-1,) + own.shape)


def scatter_stage(pieces, axes):
    size, here = lax.axis_size(axes), lax.axis_index(axes)
    return [place(pieces, here)] + [
        push(place(pieces, (here + step) & (size - 1)), axes, step) for step in range(1, size)
    ]


def sum_stage(pieces, axes):
    return sum(piece.astype(F32) for piece in scatter_stage(pieces, axes))


def reduce_row(pieces):
    shape = pieces.shape[1:]
    pieces = pieces.reshape((lax.axis_size("c"), lax.axis_size(ROW), lax.axis_size("y")) + shape)
    pieces = sum_stage(pieces, "c").astype(BF16)
    return sum_stage(pieces, ROW).astype(BF16)


def sum_plane(part):
    for axes in ("c", ROW, "y"):
        part = sum(push(part, axes, step) for step in range(lax.axis_size(axes)))
    return part


def choose_kernel(source_ref, *refs):
    parts, outs = refs[:-NWIN], refs[-NWIN:]
    count = parts[0].shape[0]
    for step, out in enumerate(outs):
        source = source_ref[step]
        for index in range(len(parts) * count):

            @pl.when(source == index)
            def _():
                out[...] = parts[index // count][index % count]


def choose(source, parts):
    whole = pl.BlockSpec(memory_space=pltpu.VMEM)
    return pl.pallas_call(
        choose_kernel,
        in_specs=[pl.BlockSpec(memory_space=pltpu.SMEM)] + [whole] * len(parts),
        out_specs=[whole] * NWIN,
        out_shape=[jax.ShapeDtypeStruct(parts[0].shape[1:], BF16)] * NWIN,
    )(source, *parts)


def fetch_window(video_q, window):
    y, x, c = (lax.axis_index(axes) for axes in ("y", ROW, "c"))
    xl_size, z_size = lax.axis_size("xl"), lax.axis_size("z")
    y_size, x_size, c_size = lax.axis_size("y"), lax.axis_size(ROW), lax.axis_size("c")
    xh_size = x_size // xl_size
    model = video_q.shape[1]

    block = lax.dynamic_slice_in_dim(
        jnp.concatenate((window, window)), y, NWIN, 0, allow_negative_indices=False
    )
    xl_of = block & (xl_size - 1)
    rest = block >> (xl_size.bit_length() - 1)
    z_of = rest & (z_size - 1)
    rest = rest >> (z_size.bit_length() - 1)
    c_of = rest & (c_size - 1)
    rest = rest >> (c_size.bit_length() - 1)
    xh_of = rest & (xh_size - 1)
    y_of = rest >> (xh_size.bit_length() - 1)
    from_x = (x - xh_of * xl_size - xl_of) & (x_size - 1)
    source = from_x * c_size + ((c - c_of) & (c_size - 1))
    from_y = (y - y_of[0]) & (y_size - 1)

    pieces = video_q.reshape(xh_size, c_size, xl_size, -1, model)

    def side(index):
        part = lax.dynamic_index_in_dim(pieces, index, 1, False, allow_negative_indices=False)
        return part.reshape(x_size, -1, model)

    pieces = jnp.stack((side(c), push(side(c ^ 1), "c", 1)), axis=1)
    chosen = choose(source, scatter_stage(pieces, ROW))
    came = [chosen[0]] + [push(chosen[step], "y", step) for step in range(1, y_size)]
    return place(jnp.stack(came), from_y), z_of[0]


def split_heads(rows, groups):
    count = rows.shape[0]
    return rows.reshape(count, groups, -1).transpose(1, 0, 2)


def merge_kernel(came_ref, k_ref, v_ref, sems):
    own = k_ref.shape[0]
    z_size, _, width = came_ref.shape
    copies = []
    for z in range(z_size):
        for part, ref in enumerate((k_ref, v_ref)):
            copies.append(
                pltpu.make_async_copy(
                    came_ref.at[z, pl.ds(part * own, own)],
                    ref.at[:, pl.ds(z * width, width)],
                    sems.at[z, part],
                )
            )
    for copy in copies:
        copy.start()
    for copy in copies:
        copy.wait()


def merge(came):
    z_size, rows, width = came.shape
    anywhere = pl.BlockSpec(memory_space=pl.ANY)
    return pl.pallas_call(
        merge_kernel,
        in_specs=[pl.BlockSpec(memory_space=pltpu.VMEM)],
        out_specs=[anywhere, anywhere],
        out_shape=[jax.ShapeDtypeStruct((rows // 2, z_size * width), BF16)] * 2,
        scratch_shapes=[pltpu.SemaphoreType.DMA((z_size, 2))],
    )(came)


def local(
    video_q, video_k, video_v, text_q, text_k, text_v,
    gain_video_q, gain_video_k, gain_text_q, gain_text_k,
    window, grad_out_video, grad_out_text,
):
    z_size = lax.axis_size("z")
    groups = lax.axis_size(PLANE)
    own_rows, model = video_q.shape
    columns = model // z_size
    heads = columns // HD
    share = grad_out_video.shape[0]
    gains = jnp.stack((gain_video_q, gain_video_k, gain_text_q, gain_text_k))

    first_v, last_v = video_v[:EARLY], video_v[EARLY:]
    moved_k = swap(split_heads(jnp.concatenate((video_k, first_v), axis=0), z_size), "z")
    picked, z_of = fetch_window(video_q, window)
    picked, moved_k = tie(picked, moved_k)
    came = swap(split_heads(picked, z_size), "z")
    own_window = place(came, z_of)
    sent_v, own_window = tie(split_heads(last_v, z_size), own_window)
    moved_v = swap(sent_v, "z")
    own = jnp.stack((own_window, text_q, grad_out_video, grad_out_text))
    own = gather_stage(gather_stage(own, "y"), ROW)
    own, moved_v = tie(own, moved_v)
    own = gather_stage(own.transpose(2, 0, 1, 3, 4), "c")
    window_rows, text_rows, *cotangent = (own[:, kind].reshape(-1, columns) for kind in range(4))
    cotangent = jnp.concatenate(cotangent, axis=0)
    operands = (window_rows, text_rows, cotangent, moved_k, moved_v, text_k, text_v)

    stats = sum_plane(attention_stats(operands, gains, heads))
    out, back, key_text, value_text = attention_grads(operands, gains, stats, heads, groups)
    back = swap(back, "z")
    total = sum_stage(reduce_row(out), "y")
    grad_video_k, grad_video_v = merge(back)

    def query_grad(raw, gain, cot):
        shape = (raw.shape[0], heads, HD)
        return pullback(raw.reshape(shape), gain, cot.reshape(shape)).reshape(raw.shape)

    return (
        total[:share].astype(BF16),
        total[share : 2 * share].astype(BF16),
        query_grad(own_window, gain_video_q, total[2 * share : 3 * share]).astype(BF16),
        query_grad(text_q, gain_text_q, total[3 * share :]).astype(BF16),
        grad_video_k,
        grad_video_v,
        key_text,
        value_text,
    )


def solution(mesh):
    fine = Mesh(mesh.devices.reshape(4, 2, 2, 8, 2), ("y", "xh", "c", "z", "xl"))
    tokens = P(("y", "xh", "c", "z", "xl"), None)
    text = P(PLANE, "z")
    return jax.shard_map(
        local,
        mesh=fine,
        in_specs=(tokens,) * 3 + (text,) * 3 + (P(),) * 5 + (text,) * 2,
        out_specs=(text,) * 4 + (tokens,) * 2 + (text,) * 2,
        check_vma=False,
    )
```

```python
import math

import jax
import jax.numpy as jnp
from jax import lax
from jax.experimental import pallas as pl
from jax.experimental.pallas import tpu as pltpu
from jax.sharding import Mesh, PartitionSpec as P

NWIN = 4
HD = 128
EPS = 1e-06
INV_ROOT = 1.0 / math.sqrt(HD)
LOG2E = math.log2(math.e)
PLANE = ("y", "xh", "c", "xl")
ROW = ("xh", "xl")
KEY_BLOCK = 1024
EARLY = 48
VMEM = 48 * 1024 * 1024
NT = (((1,), (1,)), ((), ()))
NN = (((1,), (0,)), ((), ()))
TN = (((0,), (0,)), ((), ()))
F32 = jnp.float32
BF16 = jnp.bfloat16


def mm(a, b, dims):
    return lax.dot_general(a, b, dims, preferred_element_type=F32)


def inverse_rms(rows):
    return lax.rsqrt(jnp.mean(rows * rows, axis=-1, keepdims=True) + EPS)


def normed(raw, gain):
    rows = raw.astype(F32)
    return (rows * inverse_rms(rows) * gain).astype(BF16)


def pullback(raw, gain, cot):
    rows = raw.astype(F32)
    inverse = inverse_rms(rows)
    scaled = cot * gain
    along = jnp.mean(rows * scaled, axis=-1, keepdims=True)
    return inverse * (scaled - rows * (inverse * inverse * along))


def normed_queries(win_ref, text_ref, gains_ref):
    return jnp.concatenate(
        (normed(win_ref[...], gains_ref[0:1]), normed(text_ref[...], gains_ref[2:3])), axis=0
    )


def key_parts(k_ref, v_ref, tk_ref, tv_ref, gains_ref):
    parts = []
    own = (k_ref.shape[1] + v_ref.shape[1]) // 2
    step = KEY_BLOCK // own
    for start in range(0, v_ref.shape[0], step):
        spots = slice(start, start + step)
        key = k_ref[spots, :own].reshape(KEY_BLOCK, HD)
        value = jnp.concatenate((k_ref[spots, own:], v_ref[spots]), axis=1)
        value = value.reshape(KEY_BLOCK, HD)
        parts.append((key, value, gains_ref[1:2], spots))
    parts.append((tk_ref[...], tv_ref[...], gains_ref[3:4], None))
    return parts


def stats_kernel(win_ref, tq_ref, cot_ref, k_ref, v_ref, tk_ref, tv_ref, gains_ref, out_ref):
    queries = normed_queries(win_ref, tq_ref, gains_ref)
    cot = cot_ref[...]
    den = jnp.zeros((1, queries.shape[0]), F32)
    mixed = jnp.zeros((1, queries.shape[0]), F32)
    for raw_key, value, gain, _ in key_parts(k_ref, v_ref, tk_ref, tv_ref, gains_ref):
        key = normed(raw_key, gain)
        weights = jnp.exp2(mm(key, queries, NT) * (INV_ROOT * LOG2E))
        dprobs = mm(value, cot, NT)
        den += jnp.sum(weights, axis=0, keepdims=True)
        mixed += jnp.sum(weights * dprobs, axis=0, keepdims=True)
    out_ref[0, 0:1] = den
    out_ref[0, 1:2] = mixed


def grads_kernel(
    win_ref, tq_ref, cot_ref, k_ref, v_ref, tk_ref, tv_ref, gains_ref, stats_ref,
    side_ref, own_ref, other_ref, dkv_ref, dtk_ref, dtv_ref,
):
    queries = normed_queries(win_ref, tq_ref, gains_ref)
    cot = cot_ref[...]
    count = queries.shape[0]
    inv_den = 1.0 / stats_ref[0, 0:1]
    delta = stats_ref[0, 1:2] * inv_den
    out_t = jnp.zeros((HD, count), F32)
    dq_t = jnp.zeros((HD, count), F32)
    for raw_key, value, gain, spots in key_parts(k_ref, v_ref, tk_ref, tv_ref, gains_ref):
        key = normed(raw_key, gain)
        probs = jnp.exp2(mm(key, queries, NT) * (INV_ROOT * LOG2E)) * inv_den
        probs_16 = probs.astype(BF16)
        dvalue = mm(probs_16, cot, NN).astype(BF16)
        out_t += mm(value, probs_16, TN)
        dscores = (probs * (mm(value, cot, NT) - delta)).astype(BF16)
        dkey = pullback(raw_key, gain, mm(dscores, queries, NN) * INV_ROOT).astype(BF16)
        dq_t += mm(key, dscores, TN)
        if spots is None:
            dtk_ref[...] = dkey
            dtv_ref[...] = dvalue
        else:
            own = dkv_ref.shape[1] // 2
            dkv_ref[spots, :own] = dkey.reshape(-1, own, HD)
            dkv_ref[spots, own:] = dvalue.reshape(-1, own, HD)
    half = count // 2
    outs = out_t.T
    dqs = (dq_t * INV_ROOT).T
    groups, part = own_ref.shape[0], own_ref.shape[1] // 4
    is_first = side_ref[0] == 0
    for place, block in enumerate((outs[:half], outs[half:], dqs[:half], dqs[half:])):
        low, high = block[: half // 2], block[half // 2 :]
        spot = slice(place * part, (place + 1) * part)
        for ref, rows in (
            (own_ref, jnp.where(is_first, low, high)), (other_ref, jnp.where(is_first, high, low))
        ):
            ref[:, spot] = rows.astype(BF16).reshape(groups, part, HD)


def column_spec(shape):
    lead = tuple(shape[:-1])
    return pl.BlockSpec(lead + (HD,), lambda head: (0,) * len(lead) + (head,))


PARAMS = pltpu.CompilerParams(vmem_limit_bytes=VMEM)


def operand_specs(operands, gains):
    specs = [column_spec(array.shape) for array in operands]
    return specs + [pl.BlockSpec(gains.shape, lambda head: (0, 0))]


def cost(operands, heads, dots):
    _, _, cot, moved_k, moved_v, *_ = operands
    keys = moved_k.shape[0] * (moved_k.shape[1] + moved_v.shape[1]) // 2
    work = cot.shape[0] * keys * heads
    return pl.CostEstimate(
        flops=2 * dots * work * HD, bytes_accessed=2000000 * heads, transcendentals=work
    )


def attention_stats(operands, gains, heads):
    count = operands[2].shape[0]
    return pl.pallas_call(
        stats_kernel,
        grid=(heads,),
        in_specs=operand_specs(operands, gains),
        out_specs=pl.BlockSpec((1, 2, count), lambda head: (head, 0, 0)),
        out_shape=jax.ShapeDtypeStruct((heads, 2, count), F32),
        compiler_params=PARAMS,
        cost_estimate=cost(operands, heads, 2),
    )(*operands, gains)


def attention_grads(operands, gains, stats, heads, groups):
    _, _, cot, moved_k, moved_v, text_k, _ = operands
    count = cot.shape[0]
    width = heads * HD
    rows = jax.ShapeDtypeStruct((groups // 2, count // groups * 2, width), BF16)
    shapes = [
        rows,
        rows,
        jax.ShapeDtypeStruct(
            (moved_k.shape[0], moved_k.shape[1] + moved_v.shape[1], width), BF16
        ),
        jax.ShapeDtypeStruct((text_k.shape[0], width), BF16),
        jax.ShapeDtypeStruct((text_k.shape[0], width), BF16),
    ]
    return pl.pallas_call(
        grads_kernel,
        grid=(heads,),
        in_specs=operand_specs(operands, gains)
        + [
            pl.BlockSpec((1, 2, count), lambda head: (head, 0, 0)),
            pl.BlockSpec(memory_space=pltpu.SMEM),
        ],
        out_specs=[column_spec(s.shape) for s in shapes],
        out_shape=shapes,
        compiler_params=PARAMS,
        cost_estimate=cost(operands, heads, 6),
    )(*operands, gains, stats, lax.axis_index("c")[None])


def swap(array, axes):
    return lax.all_to_all(array, axes, split_axis=0, concat_axis=0, tiled=True)


def push(array, axes, step):
    if step == 0:
        return array
    size = lax.axis_size(axes)
    return lax.ppermute(array, axes, [(i, (i + step) % size) for i in range(size)])


def place(array, index):
    return lax.dynamic_index_in_dim(array, index, 0, keepdims=False, allow_negative_indices=False)


def put(array, part, index):
    return lax.dynamic_update_index_in_dim(array, part, index, 0, allow_negative_indices=False)


def tie(*arrays):
    return lax.optimization_barrier(arrays)


def gather_stage(own, axes):
    size, here = lax.axis_size(axes), lax.axis_index(axes)
    whole = put(jnp.zeros((size,) + own.shape, own.dtype), own, here)
    for step in range(1, size):
        whole = put(whole, push(own, axes, step), (here - step) & (size - 1))
    return whole


def gather_plane(own):
    whole = gather_stage(gather_stage(gather_stage(own, "y"), ROW), "c")
    return whole.reshape((-1,) + own.shape)


def scatter_stage(pieces, axes):
    size, here = lax.axis_size(axes), lax.axis_index(axes)
    return [place(pieces, here)] + [
        push(place(pieces, (here + step) & (size - 1)), axes, step) for step in range(1, size)
    ]


def sum_stage(pieces, axes):
    return sum(piece.astype(F32) for piece in scatter_stage(pieces, axes))


def reduce_row(own, other):
    pieces = (own.astype(F32) + push(other, "c", 1).astype(F32)).astype(BF16)
    pieces = pieces.reshape((lax.axis_size(ROW), lax.axis_size("y")) + pieces.shape[1:])
    return sum_stage(pieces, ROW).astype(BF16)


def sum_plane(part):
    for axes in ("c", ROW, "y"):
        part = sum(push(part, axes, step) for step in range(lax.axis_size(axes)))
    return part


def choose_kernel(source_ref, *refs):
    parts, outs = refs[:-NWIN], refs[-NWIN:]
    count = parts[0].shape[0]
    for step, out in enumerate(outs):
        source = source_ref[step]
        for index in range(len(parts) * count):

            @pl.when(source == index)
            def _():
                out[...] = parts[index // count][index % count]


def choose(source, parts):
    whole = pl.BlockSpec(memory_space=pltpu.VMEM)
    return pl.pallas_call(
        choose_kernel,
        in_specs=[pl.BlockSpec(memory_space=pltpu.SMEM)] + [whole] * len(parts),
        out_specs=[whole] * NWIN,
        out_shape=[jax.ShapeDtypeStruct(parts[0].shape[1:], BF16)] * NWIN,
    )(source, *parts)


def fetch_window(video_q, window):
    y, x, c = (lax.axis_index(axes) for axes in ("y", ROW, "c"))
    xl_size, z_size = lax.axis_size("xl"), lax.axis_size("z")
    y_size, x_size, c_size = lax.axis_size("y"), lax.axis_size(ROW), lax.axis_size("c")
    xh_size = x_size // xl_size
    model = video_q.shape[1]

    block = lax.dynamic_slice_in_dim(
        jnp.concatenate((window, window)), y, NWIN, 0, allow_negative_indices=False
    )
    xl_of = block & (xl_size - 1)
    rest = block >> (xl_size.bit_length() - 1)
    z_of = rest & (z_size - 1)
    rest = rest >> (z_size.bit_length() - 1)
    c_of = rest & (c_size - 1)
    rest = rest >> (c_size.bit_length() - 1)
    xh_of = rest & (xh_size - 1)
    y_of = rest >> (xh_size.bit_length() - 1)
    from_x = (x - xh_of * xl_size - xl_of) & (x_size - 1)
    source = from_x * c_size + ((c - c_of) & (c_size - 1))
    from_y = (y - y_of[0]) & (y_size - 1)

    pieces = video_q.reshape(xh_size, c_size, xl_size, -1, model)

    def side(index):
        part = lax.dynamic_index_in_dim(pieces, index, 1, False, allow_negative_indices=False)
        return part.reshape(x_size, -1, model)

    pieces = jnp.stack((side(c), push(side(c ^ 1), "c", 1)), axis=1)
    chosen = choose(source, scatter_stage(pieces, ROW))
    came = [chosen[0]] + [push(chosen[step], "y", step) for step in range(1, y_size)]
    return place(jnp.stack(came), from_y), z_of[0]


def split_heads(rows, groups):
    count = rows.shape[0]
    return rows.reshape(count, groups, -1).transpose(1, 0, 2)


def merge_kernel(came_ref, k_ref, v_ref, sems):
    own = k_ref.shape[0]
    z_size, _, width = came_ref.shape
    copies = []
    for z in range(z_size):
        for part, ref in enumerate((k_ref, v_ref)):
            copies.append(
                pltpu.make_async_copy(
                    came_ref.at[z, pl.ds(part * own, own)],
                    ref.at[:, pl.ds(z * width, width)],
                    sems.at[z, part],
                )
            )
    for copy in copies:
        copy.start()
    for copy in copies:
        copy.wait()


def merge(came):
    z_size, rows, width = came.shape
    anywhere = pl.BlockSpec(memory_space=pl.ANY)
    return pl.pallas_call(
        merge_kernel,
        in_specs=[pl.BlockSpec(memory_space=pltpu.VMEM)],
        out_specs=[anywhere, anywhere],
        out_shape=[jax.ShapeDtypeStruct((rows // 2, z_size * width), BF16)] * 2,
        scratch_shapes=[pltpu.SemaphoreType.DMA((z_size, 2))],
    )(came)


def local(
    video_q, video_k, video_v, text_q, text_k, text_v,
    gain_video_q, gain_video_k, gain_text_q, gain_text_k,
    window, grad_out_video, grad_out_text,
):
    z_size = lax.axis_size("z")
    groups = lax.axis_size(PLANE)
    own_rows, model = video_q.shape
    columns = model // z_size
    heads = columns // HD
    share = grad_out_video.shape[0]
    gains = jnp.stack((gain_video_q, gain_video_k, gain_text_q, gain_text_k))

    first_v, last_v = video_v[:EARLY], video_v[EARLY:]
    moved_k = swap(split_heads(jnp.concatenate((video_k, first_v), axis=0), z_size), "z")
    picked, z_of = fetch_window(video_q, window)
    picked, moved_k = tie(picked, moved_k)
    came = swap(split_heads(picked, z_size), "z")
    own_window = place(came, z_of)
    sent_v, own_window = tie(split_heads(last_v, z_size), own_window)
    moved_v = swap(sent_v, "z")
    own = jnp.stack((own_window, text_q, grad_out_video, grad_out_text))
    own = gather_stage(gather_stage(own, "y"), ROW)
    own, moved_v = tie(own, moved_v)
    own = gather_stage(own.transpose(2, 0, 1, 3, 4), "c")
    window_rows, text_rows, *cotangent = (own[:, kind].reshape(-1, columns) for kind in range(4))
    cotangent = jnp.concatenate(cotangent, axis=0)
    operands = (window_rows, text_rows, cotangent, moved_k, moved_v, text_k, text_v)

    stats = sum_plane(attention_stats(operands, gains, heads))
    out, other, back, key_text, value_text = attention_grads(operands, gains, stats, heads, groups)
    back = swap(back, "z")
    total = sum_stage(reduce_row(out, other), "y")
    grad_video_k, grad_video_v = merge(back)

    def query_grad(raw, gain, cot):
        shape = (raw.shape[0], heads, HD)
        return pullback(raw.reshape(shape), gain, cot.reshape(shape)).reshape(raw.shape)

    return (
        total[:share].astype(BF16),
        total[share : 2 * share].astype(BF16),
        query_grad(own_window, gain_video_q, total[2 * share : 3 * share]).astype(BF16),
        query_grad(text_q, gain_text_q, total[3 * share :]).astype(BF16),
        grad_video_k,
        grad_video_v,
        key_text,
        value_text,
    )


def solution(mesh):
    fine = Mesh(mesh.devices.reshape(4, 2, 2, 8, 2), ("y", "xh", "c", "z", "xl"))
    tokens = P(("y", "xh", "c", "z", "xl"), None)
    text = P(PLANE, "z")
    return jax.shard_map(
        local,
        mesh=fine,
        in_specs=(tokens,) * 3 + (text,) * 3 + (P(),) * 5 + (text,) * 2,
        out_specs=(text,) * 4 + (tokens,) * 2 + (text,) * 2,
        check_vma=False,
    )
```
